256 devices in a mesh: kvp: 32 (over x, y, core), tp: 8 (over z).
Axes of the slice: x: 4, y: 4, z: 8, core: 2. Of those that a mesh axis runs over, the one named last changes fastest.
Arguments:
- residual: bfloat16 [8, 16384], P(None, ('kvp', 'tp')), may hold values from -10 to 10
- norm_gain: bfloat16 [16384], P(('kvp', 'tp')), may hold values from 0.25 to 1.75
- queries: bfloat16 [8, 128, 128], P(None, 'tp'), may hold values from -100 to 100
- keys: bfloat16 [8, 4096, 8, 128], P(None, 'kvp', 'tp'), may hold values from -4 to 4
- values: bfloat16 [8, 4096, 8, 128], P(None, 'kvp', 'tp'), may hold values from -12 to 12
- new_kv: bfloat16 [8, 2, 8, 128], P(None, None, 'tp'), may hold values from -8 to 8
- lens: int32 [8], replicated, may hold values from 2 to 4096, as said below
- out_weight: bfloat16 [16384, 16384], P('tp', 'kvp'), may hold values from -0.09375 to 0.09375
- gate_weight: bfloat16 [26624, 16384], P(('kvp', 'tp')), may hold values from -0.046875 to 0.046875
- up_weight: bfloat16 [26624, 16384], P(('kvp', 'tp')), may hold values from -0.046875 to 0.046875
- down_weight: bfloat16 [26624, 16384], P(('kvp', 'tp')), may hold values from -0.15625 to 0.15625
Outputs:
- layer_out: bfloat16 [8, 16384], P(None, ('kvp', 'tp'))
The draws below stay inside these ranges and needn't reach their ends.
Inputs may be any that keep to these rules, and one draw needn't show every extreme that they name: `lens`: one request has exactly 4096 positions in use.
All inputs are finite; a program needn't handle non-finite values.
Results may differ from the reference program's by a relative error of at most 0.02.
Values may be sent and summed in bfloat16 or wider, within the bound.
A program may use at most 64 MiB of HBM per device.

```python
import math
import jax
import jax.numpy as jnp
from jax import lax

D = 16384
HQ = 128
KVH = 8
HD = 128
FF = 26624
B = 8
CTX = 4096


def shared_keys(key):
    base = jax.random.normal(jax.random.fold_in(key, 11), (B, CTX, KVH, HD), jnp.float32)
    return jnp.clip(base, -4.0, 4.0)


def draw_keys(key, part):
    base = shared_keys(key)
    return base.astype(jnp.bfloat16)


def draw_queries(key, part):
    key = jax.random.fold_in(key, 5)
    key_drawn = jax.random.fold_in(key, 0)
    drawn = jnp.clip(jax.random.normal(key_drawn, (B, HQ, HD), jnp.float32), -4.0, 4.0)
    return drawn.astype(jnp.bfloat16)


def draw_lens(key, part):
    key = jax.random.fold_in(key, 7)
    key_lens, key_spot = jax.random.split(key)
    counts = jax.random.randint(key_lens, (B,), 2, CTX + 1, dtype=jnp.int32)
    chosen = jax.random.randint(key_spot, (), 0, B, dtype=jnp.int32)
    return jnp.where(jnp.arange(B, dtype=jnp.int32) == chosen, CTX, counts).astype(jnp.int32)


def draw_residual(key, part):
    key = jax.random.fold_in(key, 9)
    key_noise, key_spread, key_rows = jax.random.split(key, 3)
    columns = jnp.arange(D, dtype=jnp.float32) / (D - 1)
    trend = jnp.exp(columns * math.log(3.0))
    spread = jnp.exp(jax.random.uniform(key_spread, (D,), jnp.float32) * math.log(3.4))
    noise = jnp.clip(jax.random.normal(key_noise, (B, D), jnp.float32), -3.0, 3.0)
    rows = jnp.exp(jax.random.uniform(key_rows, (B, 1), jnp.float32, math.log(0.5), math.log(1.5)))
    return (noise * trend * spread * rows * 0.15).astype(jnp.bfloat16)


def spiked(result, key, source, target, shards_of, factor):
    def block_of(position):
        return (jnp.arange(result.shape[position]) // (result.shape[position] // shards_of)).reshape((-1,) + (1,) * (result.ndim - 1 - position))

    one_side = jax.random.permutation(key, shards_of)[block_of(target)]
    far = (block_of(target) + shards_of // 2) % shards_of
    return jnp.where((block_of(source) == one_side) | (block_of(source) == far), factor * result, result)


def block_scale(stream_key, shape, shards, least, top_value):
    def one(position, blocks):
        heights = jax.random.uniform(jax.random.fold_in(jax.random.fold_in(stream_key, 6), position), (blocks,), jnp.float32, least / len(shards), top_value / len(shards))
        return jnp.repeat(jnp.exp(heights), shape[position] // blocks).reshape((-1,) + (1,) * (len(shape) - position - 1))

    factor_of = one(*shards[0])
    for cut in shards[1:]:
        factor_of = factor_of * one(*cut)
    return factor_of


def bell_draw(stream_key, shape, width, most, pieces=(), held_as=jnp.bfloat16):
    level = block_scale(stream_key, shape, pieces, -0.22, 0.18) if pieces else 1.0
    drawn = jax.random.normal(stream_key, shape, jnp.float32) * width * level
    return jnp.minimum(jnp.maximum(drawn, -most), most).astype(held_as)


def noise_with(rng, dims, width, limit, cuts, heavy, held_as=jnp.bfloat16):
    array = width * jax.random.normal(rng, dims, jnp.float32)
    if cuts:
        array = array * block_scale(rng, dims, cuts, -0.22, 0.18)
    return jnp.clip(spiked(array, jax.random.fold_in(rng, 3), *heavy), -limit, limit).astype(held_as)


def setup_inputs(seed: int = 0) -> dict:
    splits = jax.random.split(jax.random.key(seed), 12)
    residual = draw_residual(jax.random.fold_in(splits[11], 71), 0)
    norm_gain = jnp.clip(1.0 + 0.15 * jax.random.normal(splits[1], (D,), jnp.float32), 0.25, 1.75).astype(jnp.bfloat16)
    queries = draw_queries(jax.random.fold_in(splits[11], 71), 0)
    keys = draw_keys(jax.random.fold_in(splits[11], 71), 0)
    values = bell_draw(splits[4], (B, CTX, KVH, HD), 3.0, 12.0, ((1, 32), (2, 8)))
    new_kv = bell_draw(splits[5], (B, 2, KVH, HD), 2.0, 8.0, ((2, 8),))
    lens = draw_lens(jax.random.fold_in(splits[11], 71), 0)
    out_weight = noise_with(splits[7], (HQ * HD, D), (HQ * HD) ** -0.5, 0.09375, ((0, 8), (1, 32)), (0, 1, 32, 2.75))
    gate_weight = bell_draw(splits[8], (FF, D), D ** -0.5, 0.046875, ((0, 256),))
    up_weight = bell_draw(splits[9], (FF, D), D ** -0.5, 0.046875, ((0, 256),))
    down_weight = noise_with(splits[10], (FF, D), FF ** -0.5, 0.15625, ((0, 256),), (0, 1, 256, 6.0))
    return dict(residual=residual, norm_gain=norm_gain, queries=queries, keys=keys, values=values, new_kv=new_kv, lens=lens, out_weight=out_weight, gate_weight=gate_weight, up_weight=up_weight, down_weight=down_weight)


def reference(residual, norm_gain, queries, keys, values, new_kv, lens, out_weight, gate_weight, up_weight, down_weight):
    group_size = HQ // KVH
    score_scale = 1.0 / math.sqrt(HD)
    grouped = queries.astype(jnp.float32).reshape(B, KVH, group_size, HD)
    scores = jnp.einsum('bgqd,bcgd->bgqc', grouped, keys.astype(jnp.float32)) * score_scale
    visible = jnp.arange(CTX, dtype=jnp.int32)[None, :] < lens[:, None]
    visible_mask = visible[:, None, None, :]
    scores = jnp.where(visible_mask, scores, -1e+30)
    new_keys = new_kv[:, 0].astype(jnp.float32)
    new_values = new_kv[:, 1].astype(jnp.float32)
    fresh = jnp.einsum('bgqd,bgd->bgq', grouped, new_keys) * score_scale
    top_score = jnp.maximum(lax.optimization_barrier(jnp.max(scores, axis=-1)), fresh)
    weights = jnp.where(visible_mask, jnp.exp(scores - top_score[..., None]), 0.0)
    fresh_weight = jnp.exp(fresh - top_score)
    totals = lax.optimization_barrier(jnp.sum(weights, axis=-1)) + fresh_weight
    summed = jnp.einsum('bgqc,bcgd->bgqd', weights, values.astype(jnp.float32), precision=lax.Precision.HIGHEST)
    summed = summed + fresh_weight[..., None] * new_values[:, :, None, :]
    attended = (summed / totals[..., None]).reshape(B, HQ * HD).astype(jnp.bfloat16)
    projected = jnp.dot(attended, out_weight, preferred_element_type=jnp.float32)
    hidden_state = (residual.astype(jnp.float32) + projected).astype(jnp.bfloat16)
    hidden_float = hidden_state.astype(jnp.float32)
    mean_square = lax.optimization_barrier(jnp.mean(hidden_float * hidden_float, axis=-1, keepdims=True))
    normed = (hidden_float * lax.rsqrt(mean_square + 1e-05) * norm_gain.astype(jnp.float32)).astype(jnp.bfloat16)
    contract = (((1,), (1,)), ((), ()))
    gate = lax.dot_general(normed, gate_weight, contract, preferred_element_type=jnp.float32)
    upward = lax.dot_general(normed, up_weight, contract, preferred_element_type=jnp.float32)
    inner = (jax.nn.silu(gate) * upward).astype(jnp.bfloat16)
    feed_out = jnp.dot(inner, down_weight, preferred_element_type=jnp.float32)
    return (hidden_float + feed_out).astype(jnp.bfloat16)
```

```python
import functools
import math

import jax
import jax.numpy as jnp
from jax import lax
from jax.experimental import pallas as pl
from jax.experimental.pallas import tpu as pltpu
from jax.sharding import PartitionSpec as P

MESH = pl.DeviceIdType.MESH
BF = jnp.bfloat16
F32 = jnp.float32
D = 16384
EPS = 1e-05
EMPTY = -1e30
X, Y, C, Z = 4, 4, 2, 8
KVP = X * Y * C


def hops(dx, dy):
    return min(dx, X - dx) + min(dy, Y - dy)


ROW = sorted([(dx, 0, dc) for dx in range(X) for dc in range(C)][1:], key=lambda o: -hops(o[0], o[1]))
COL = sorted([(0, dy, dc) for dy in range(Y) for dc in range(C)][1:], key=lambda o: -hops(o[0], o[1]))
PLANE = sorted(
    [(dx, dy, dc) for dx in range(X) for dy in range(Y) for dc in range(C)][1:],
    key=lambda o: (-hops(o[0], o[1]), -o[2]),
)
DEPTH = sorted(range(1, Z), key=lambda dz: -min(dz, Z - dz))


def pack(ref, o, m, l):
    rows = lax.broadcasted_iota(jnp.int32, (16, 128), 0)
    high = l.astype(BF).astype(F32)
    tail = jnp.where(rows == 0, m, jnp.where(rows == 1, high, jnp.where(rows == 2, l - high, 0.0)))
    ref[pl.ds(0, 64), :] = o.astype(BF)
    ref[pl.ds(64, 16), :] = tail.astype(BF)


def unpack(x):
    o = x[0:64].astype(F32)
    tail = x[64:80].astype(F32)
    return o, tail[0:1], tail[1:2] + tail[2:3]


def combine(parts):
    m = functools.reduce(jnp.maximum, [p[1] for p in parts])
    o, l = 0.0, 0.0
    for po, pm, pl_ in parts:
        factor = jnp.exp(pm - m)
        o = o + po * factor
        l = l + pl_ * factor
    return o, m, l


def kernel(
    res_h, gain_h, q_h, k_h, v_h, nkv_h, lens_h, ow_h, gw_h, uw_h, dw_h,
    out_ref,
    res_v, gain_v, q_v, k_v, v_v, nkv_v, lens_s, ow_v, gw_v, uw_v, dw_v,
    row_send, row_recv, col_send, col_recv, side_send, side_recv,
    proj_send, proj_recv, norm_send, norm_recv, down_send, down_recv, last_send, last_recv,
    load_sem, send_sem, recv_sem, norm_sem,
):
    kvp = lax.axis_index("kvp")
    z = lax.axis_index("tp")
    x = kvp // (Y * C)
    y = lax.rem(kvp // C, Y)
    c = lax.rem(kvp, C)
    xs = [x] + [lax.rem(x + d, X) for d in range(1, X)]
    ys = [y] + [lax.rem(y + d, Y) for d in range(1, Y)]
    cs = [c, 1 - c]
    zs = [z] + [lax.rem(z + d, Z) for d in range(1, Z)]

    def index(o):
        return (xs[o[0]] * Y + ys[o[1]]) * C + cs[o[2]]

    def origin(o):
        return index(((X - o[0]) % X, (Y - o[1]) % Y, (C - o[2]) % C))

    small = [(k_h, k_v), (q_h, q_v), (v_h, v_v), (nkv_h, nkv_v), (lens_h, lens_s), (res_h, res_v), (gain_h, gain_v)]
    large = [(ow_h, ow_v), (gw_h, gw_v), (uw_h, uw_v), (dw_h, dw_v)]
    small = [pltpu.make_async_copy(s, d, load_sem.at[i]) for i, (s, d) in enumerate(small)]
    large = [pltpu.make_async_copy(s, d, load_sem.at[7 + i]) for i, (s, d) in enumerate(large)]
    for copy in small:
        copy.start()

    barrier = pltpu.get_barrier_semaphore()
    for dz in DEPTH:
        pl.semaphore_signal(barrier, inc=1, device_id=(kvp, zs[dz]), device_id_type=MESH)
    for o in PLANE:
        pl.semaphore_signal(barrier, inc=1, device_id=(index(o), z), device_id_type=MESH)

    for copy in small:
        copy.wait()
    for copy in large:
        copy.start()

    scale = 1.0 / math.sqrt(128)
    ri = lax.broadcasted_iota(jnp.int32, (128, 128), 0)
    li = lax.broadcasted_iota(jnp.int32, (128, 128), 1)
    perm = (li == (ri & 7) * 16 + (ri >> 3)).astype(BF)
    q = jnp.dot(perm, q_v[...].reshape(128, 128), preferred_element_type=F32)
    qm = jnp.concatenate([jnp.where((ri & 7) == b, q, 0.0).astype(BF) for b in range(8)], axis=1)
    kc = jnp.concatenate([k_v[b] for b in range(8)], axis=1)
    nkv = nkv_v[...].astype(F32)
    nk = nkv[:, 0, :]
    nv = nkv[:, 1, :]
    nkc = jnp.concatenate([jnp.broadcast_to(nk[b : b + 1], (8, 128)) for b in range(8)], axis=1).astype(BF)
    contract = (((1,), (1,)), ((), ()))
    s = lax.dot_general(kc, qm, contract, preferred_element_type=F32) * scale
    fresh = lax.dot_general(nkc, qm, contract, preferred_element_type=F32)[0:1] * scale
    lane = lax.broadcasted_iota(jnp.int32, (1, 128), 1) & 7
    limit = functools.reduce(lambda a, b: jnp.where(lane == b, lens_s[b], a), range(1, 8), jnp.full((1, 128), lens_s[0]))
    live = (ri + kvp * 128) < limit
    mine = (jnp.zeros((1, 128), jnp.int32) + kvp) == 0
    s = jnp.where(live, s, EMPTY)
    fresh = jnp.where(mine, fresh, EMPTY)
    m = jnp.maximum(jnp.max(s, axis=0, keepdims=True), fresh)
    m = m.astype(BF).astype(F32)
    p = jnp.where(live, jnp.exp(s - m), 0.0)
    pf = jnp.where(mine, jnp.exp(fresh - m), 0.0)
    l = jnp.sum(p, axis=0, keepdims=True) + pf
    pm = jnp.concatenate([jnp.where((li & 7) == b, p, 0.0).astype(BF) for b in range(8)], axis=0)
    vt = jnp.concatenate([v_v[b].T for b in range(8)], axis=1)
    o = jnp.dot(vt, pm, preferred_element_type=F32)
    ri8 = lax.broadcasted_iota(jnp.int32, (8, 128), 0)
    li8 = lax.broadcasted_iota(jnp.int32, (8, 128), 1)
    pfm = jnp.where((li8 & 7) == ri8, pf, 0.0)
    pad = jnp.zeros((120, 128), F32)
    nvt = jnp.concatenate([nv, pad], axis=0).T.astype(BF)
    o = o + jnp.dot(nvt, jnp.concatenate([pfm, pad], axis=0).astype(BF), preferred_element_type=F32)
    pack(row_send.at[0], o[0:64], m, l)
    pack(row_send.at[1], o[64:128], m, l)
    side_send[...] = jnp.concatenate(
        [res_v[...], jnp.broadcast_to(gain_v[...].astype(F32).reshape(1, 64), (8, 64)).astype(BF)], axis=1
    )

    pl.semaphore_wait(barrier, len(PLANE) + len(DEPTH))

    def send(src, dst, sends, recvs, device):
        pltpu.make_async_remote_copy(src, dst, sends, recvs, device_id=device, device_id_type=MESH).start()

    def whole(ref, sem):
        pltpu.make_async_copy(ref, ref, sem).wait()

    for j, o_ in enumerate(ROW):
        send(row_send.at[cs[o_[2]]], row_recv.at[j], send_sem.at[0], recv_sem.at[0], (index(o_), z))
    for j, dz in enumerate(DEPTH):
        send(side_send, side_recv.at[j], send_sem.at[1], recv_sem.at[1], (kvp, zs[dz]))
    whole(row_recv, recv_sem.at[0])
    o, m, l = combine([unpack(row_send[c])] + [unpack(row_recv[j]) for j in range(len(ROW))])
    pack(col_send, o, m, l)

    for j, o_ in enumerate(COL):
        send(col_send, col_recv.at[j], send_sem.at[2], recv_sem.at[2], (index(o_), z))
    whole(side_recv, recv_sem.at[1])
    lane8 = lax.broadcasted_iota(jnp.int32, (8, 128), 1)
    low = lane8 < 64
    side = [side_send[...].astype(F32)] + [side_recv[j].astype(F32) for j in range(Z - 1)]
    owner = [z] + [zs[Z - dz] for dz in DEPTH]
    res_parts, gain_parts = [], []
    for g in range(Z // 2):
        r, gn = jnp.zeros((8, 128), F32), jnp.zeros((8, 128), F32)
        for t, own in zip(side, owner):
            turned = pltpu.roll(t, 64, 1)
            here = (jnp.zeros((8, 128), jnp.int32) + own) == jnp.where(low, 2 * g, 2 * g + 1)
            r = jnp.where(here, jnp.where(low, t, turned), r)
            gn = jnp.where(here, jnp.where(low, turned, t), gn)
        res_parts.append(r)
        gain_parts.append(gn)
    res = jnp.concatenate(res_parts, axis=1)
    gain = jnp.concatenate(gain_parts, axis=1)
    whole(col_recv, recv_sem.at[2])
    own = [unpack(col_send[...])] + [unpack(col_recv[j]) for j, o_ in enumerate(COL) if o_[2] == 0]
    other = [unpack(col_recv[j]) for j, o_ in enumerate(COL) if o_[2] == 1]
    o, _, l = combine(own)
    own = o / l
    o, _, l = combine(other)
    other = o / l
    first = (jnp.zeros((64, 128), jnp.int32) + c) == 0
    att = jnp.concatenate([jnp.where(first, own, other), jnp.where(first, other, own)], axis=0).T
    att = jnp.concatenate([att[8 * h : 8 * h + 8] for h in range(16)], axis=1).astype(BF)

    large[0].wait()
    part = jnp.dot(att, ow_v[...], preferred_element_type=F32)
    proj_send[...] = part.astype(BF)
    for j, dz in enumerate(DEPTH):
        send(proj_send, proj_recv.at[j], send_sem.at[3], recv_sem.at[3], (kvp, zs[dz]))
    whole(proj_recv, recv_sem.at[3])
    total = part
    for j in range(Z - 1):
        total = total + proj_recv[j].astype(F32)
    hidden = (res + total).astype(BF).astype(F32)
    square = jnp.sum(hidden * hidden, axis=1, keepdims=True)
    high = square.astype(BF).astype(F32)
    norm_send[:, pl.ds(0, 512)] = (hidden * gain).astype(BF)
    norm_send[:, pl.ds(512, 128)] = jnp.where(low, high, square - high).astype(BF)

    for j, o_ in enumerate(PLANE):
        send(norm_send, norm_recv.at[j], send_sem.at[4], norm_sem.at[j], (index(o_), z))
    for copy in large[1:3]:
        copy.wait()

    def gate_up(ref, block, gate, up):
        feats = ref[:, pl.ds(0, 512)]
        cols = pl.ds(pl.multiple_of(block * 512, 512), 512)
        gate = gate + lax.dot_general(feats, gw_v[:, cols], contract, preferred_element_type=F32)
        up = up + lax.dot_general(feats, uw_v[:, cols], contract, preferred_element_type=F32)
        return gate, up, ref[:, pl.ds(512, 128)].astype(F32)

    gate = jnp.zeros((8, 104), F32)
    up = jnp.zeros((8, 104), F32)
    gate, up, squares = gate_up(norm_send, kvp, gate, up)
    for j in reversed(range(len(PLANE))):
        slot = norm_recv.at[j]
        whole(slot, norm_sem.at[j])
        gate, up, extra = gate_up(slot, origin(PLANE[j]), gate, up)
        squares = squares + extra
    squares = squares[:, 0:1] + squares[:, 64:65]
    inverse = lax.rsqrt(squares * (1.0 / D) + EPS)
    gate = gate * inverse
    up = up * inverse
    inner = (gate / (1.0 + jnp.exp(-gate)) * up).astype(BF)

    large[3].wait()

    def down(block):
        cols = pl.ds(pl.multiple_of(block * 512, 512), 512)
        return jnp.dot(inner, dw_v[:, cols], preferred_element_type=F32)

    for j, o_ in enumerate(PLANE):
        down_send[j] = down(index(o_)).astype(BF)
        send(down_send.at[j], down_recv.at[j], send_sem.at[5], recv_sem.at[4], (index(o_), z))
    total = down(kvp)
    whole(down_recv, recv_sem.at[4])
    for j in range(len(PLANE)):
        total = total + down_recv[j].astype(F32)

    for g in range(Z // 2):
        last_send[g] = total[:, 128 * g : 128 * g + 128]
    for j, dz in enumerate(DEPTH):
        send(last_send.at[zs[dz] // 2], last_recv.at[j], send_sem.at[6], recv_sem.at[5], (kvp, zs[dz]))
    mine = last_send[z // 2]
    hid = jnp.zeros((8, 128), F32)
    for g in range(Z // 2):
        hid = jnp.where((jnp.zeros((8, 128), jnp.int32) + z // 2) == g, hidden[:, 128 * g : 128 * g + 128], hid)
    whole(last_recv, recv_sem.at[5])
    for j in range(Z - 1):
        mine = mine + last_recv[j]
    mine = mine + hid
    odd = (jnp.zeros((8, 128), jnp.int32) + lax.rem(z, 2)) == 1
    mine = jnp.where(odd, pltpu.roll(mine, 64, 1), mine)
    out_ref[...] = mine[:, 0:64].astype(BF)

    for i, ref in enumerate((row_recv, side_recv, col_recv, proj_recv, norm_recv, down_recv, last_recv)):
        whole(ref, send_sem.at[i])


def local(residual, norm_gain, queries, keys, values, new_kv, lens, out_weight, gate_weight, up_weight, down_weight):
    V = pltpu.VMEM
    n = len(PLANE)
    scratch = [
        V((8, 64), BF), V((64,), BF), V((8, 16, 128), BF), V((8, 128, 128), BF), V((8, 128, 128), BF),
        V((8, 2, 128), BF), pltpu.SMEM((8,), jnp.int32), V((2048, 512), BF),
        V((104, D), BF), V((104, D), BF), V((104, D), BF),
        V((2, 80, 128), BF), V((7, 80, 128), BF), V((80, 128), BF), V((7, 80, 128), BF),
        V((8, 128), BF), V((7, 8, 128), BF),
        V((8, 512), BF), V((7, 8, 512), BF), V((8, 640), BF), V((n, 8, 640), BF),
        V((n, 8, 512), BF), V((n, 8, 512), BF), V((4, 8, 128), F32), V((7, 8, 128), F32),
        pltpu.SemaphoreType.DMA((11,)), pltpu.SemaphoreType.DMA((7,)), pltpu.SemaphoreType.DMA((6,)),
        pltpu.SemaphoreType.DMA((n,)),
    ]
    return pl.pallas_call(
        kernel,
        name="decode_step",
        out_shape=jax.ShapeDtypeStruct((8, 64), BF),
        in_specs=[pl.BlockSpec(memory_space=pl.ANY)] * 11,
        out_specs=pl.BlockSpec(memory_space=pltpu.VMEM),
        scratch_shapes=scratch,
        cost_estimate=pl.CostEstimate(flops=120_000_000, bytes_accessed=13_000_000, transcendentals=20_000),
        compiler_params=pltpu.CompilerParams(collective_id=0, has_side_effects=True, vmem_limit_bytes=48 << 20),
    )(
        residual, norm_gain, queries, keys.reshape(8, 128, 128), values.reshape(8, 128, 128),
        new_kv.reshape(8, 2, 128), lens, out_weight, gate_weight, up_weight, down_weight,
    )


def solution(mesh):
    in_specs = (
        P(None, ("kvp", "tp")),
        P(("kvp", "tp")),
        P(None, "tp", None),
        P(None, "kvp", "tp", None),
        P(None, "kvp", "tp", None),
        P(None, None, "tp", None),
        P(),
        P("tp", "kvp"),
        P(("kvp", "tp"), None),
        P(("kvp", "tp"), None),
        P(("kvp", "tp"), None),
    )
    out_specs = P(None, ("kvp", "tp"))
    return jax.shard_map(local, mesh=mesh, in_specs=in_specs, out_specs=out_specs, check_vma=False)
```

```python
import functools
import math

import jax
import jax.numpy as jnp
from jax import lax
from jax.experimental import pallas as pl
from jax.experimental.pallas import tpu as pltpu
from jax.sharding import PartitionSpec as P

MESH = pl.DeviceIdType.MESH
BF = jnp.bfloat16
F32 = jnp.float32
D = 16384
EPS = 1e-05
EMPTY = -1e30
X, Y, C, Z = 4, 4, 2, 8
KVP = X * Y * C


def hops(dx, dy):
    return min(dx, X - dx) + min(dy, Y - dy)


ROW = sorted([(dx, 0, dc) for dx in range(X) for dc in range(C)][1:], key=lambda o: -hops(o[0], o[1]))
COL = sorted([(0, dy, dc) for dy in range(Y) for dc in range(C)][1:], key=lambda o: -hops(o[0], o[1]))
PLANE = sorted(
    [(dx, dy, dc) for dx in range(X) for dy in range(Y) for dc in range(C)][1:],
    key=lambda o: (-hops(o[0], o[1]), -o[2]),
)
CHIPS = [o for o in PLANE if o[2] == 0]
GROUP = 4
DEPTH = sorted(range(1, Z), key=lambda dz: -min(dz, Z - dz))


def pack(ref, o, m, l):
    rows = lax.broadcasted_iota(jnp.int32, (16, 128), 0)
    high = l.astype(BF).astype(F32)
    tail = jnp.where(rows == 0, m, jnp.where(rows == 1, high, jnp.where(rows == 2, l - high, 0.0)))
    ref[pl.ds(0, 64), :] = o.astype(BF)
    ref[pl.ds(64, 16), :] = tail.astype(BF)


def unpack(x):
    o = x[0:64].astype(F32)
    tail = x[64:80].astype(F32)
    return o, tail[0:1], tail[1:2] + tail[2:3]


def combine(parts):
    m = functools.reduce(jnp.maximum, [p[1] for p in parts])
    o, l = 0.0, 0.0
    for po, pm, pl_ in parts:
        factor = jnp.exp(pm - m)
        o = o + po * factor
        l = l + pl_ * factor
    return o, m, l


def kernel(
    res_h, gain_h, q_h, k_h, v_h, nkv_h, lens_h, ow_h, gw_h, uw_h, dw_h,
    out_ref,
    res_v, gain_v, q_v, k_v, v_v, nkv_v, lens_s, ow_v, gw_v, uw_v, dw_v,
    row_send, row_recv, col_send, col_recv, side_send, side_recv,
    proj_send, proj_recv, norm_send, norm_recv, pass_recv, pair_send, pair_recv, down_send, down_recv, last_send, last_recv,
    load_sem, send_sem, recv_sem, norm_sem, pair_sem,
):
    kvp = lax.axis_index("kvp")
    z = lax.axis_index("tp")
    x = kvp // (Y * C)
    y = lax.rem(kvp // C, Y)
    c = lax.rem(kvp, C)
    xs = [x] + [lax.rem(x + d, X) for d in range(1, X)]
    ys = [y] + [lax.rem(y + d, Y) for d in range(1, Y)]
    cs = [c, 1 - c]
    zs = [z] + [lax.rem(z + d, Z) for d in range(1, Z)]

    def index(o):
        return (xs[o[0]] * Y + ys[o[1]]) * C + cs[o[2]]

    def origin(o):
        return index(((X - o[0]) % X, (Y - o[1]) % Y, (C - o[2]) % C))

    small = [(k_h, k_v), (q_h, q_v), (v_h, v_v), (nkv_h, nkv_v), (lens_h, lens_s), (res_h, res_v), (gain_h, gain_v)]
    large = [(ow_h, ow_v), (gw_h, gw_v), (uw_h, uw_v), (dw_h, dw_v)]
    small = [pltpu.make_async_copy(s, d, load_sem.at[i]) for i, (s, d) in enumerate(small)]
    large = [pltpu.make_async_copy(s, d, load_sem.at[7 + i]) for i, (s, d) in enumerate(large)]
    for copy in small:
        copy.start()

    barrier = pltpu.get_barrier_semaphore()
    for dz in DEPTH:
        pl.semaphore_signal(barrier, inc=1, device_id=(kvp, zs[dz]), device_id_type=MESH)
    for o in PLANE:
        pl.semaphore_signal(barrier, inc=1, device_id=(index(o), z), device_id_type=MESH)

    for copy in small:
        copy.wait()
    for copy in large:
        copy.start()

    scale = 1.0 / math.sqrt(128)
    ri = lax.broadcasted_iota(jnp.int32, (128, 128), 0)
    li = lax.broadcasted_iota(jnp.int32, (128, 128), 1)
    perm = (li == (ri & 7) * 16 + (ri >> 3)).astype(BF)
    q = jnp.dot(perm, q_v[...].reshape(128, 128), preferred_element_type=F32)
    qm = jnp.concatenate([jnp.where((ri & 7) == b, q, 0.0).astype(BF) for b in range(8)], axis=1)
    kc = jnp.concatenate([k_v[b] for b in range(8)], axis=1)
    nkv = nkv_v[...].astype(F32)
    nk = nkv[:, 0, :]
    nv = nkv[:, 1, :]
    nkc = jnp.concatenate([jnp.broadcast_to(nk[b : b + 1], (8, 128)) for b in range(8)], axis=1).astype(BF)
    contract = (((1,), (1,)), ((), ()))
    s = lax.dot_general(kc, qm, contract, preferred_element_type=F32) * scale
    fresh = lax.dot_general(nkc, qm, contract, preferred_element_type=F32)[0:1] * scale
    lane = lax.broadcasted_iota(jnp.int32, (1, 128), 1) & 7
    limit = functools.reduce(lambda a, b: jnp.where(lane == b, lens_s[b], a), range(1, 8), jnp.full((1, 128), lens_s[0]))
    live = (ri + kvp * 128) < limit
    mine = (jnp.zeros((1, 128), jnp.int32) + kvp) == 0
    s = jnp.where(live, s, EMPTY)
    fresh = jnp.where(mine, fresh, EMPTY)
    m = jnp.maximum(jnp.max(s, axis=0, keepdims=True), fresh)
    m = m.astype(BF).astype(F32)
    p = jnp.where(live, jnp.exp(s - m), 0.0)
    pf = jnp.where(mine, jnp.exp(fresh - m), 0.0)
    l = jnp.sum(p, axis=0, keepdims=True) + pf
    pm = jnp.concatenate([jnp.where((li & 7) == b, p, 0.0).astype(BF) for b in range(8)], axis=0)
    vt = jnp.concatenate([v_v[b].T for b in range(8)], axis=1)
    o = jnp.dot(vt, pm, preferred_element_type=F32)
    ri8 = lax.broadcasted_iota(jnp.int32, (8, 128), 0)
    li8 = lax.broadcasted_iota(jnp.int32, (8, 128), 1)
    pfm = jnp.where((li8 & 7) == ri8, pf, 0.0)
    pad = jnp.zeros((120, 128), F32)
    nvt = jnp.concatenate([nv, pad], axis=0).T.astype(BF)
    o = o + jnp.dot(nvt, jnp.concatenate([pfm, pad], axis=0).astype(BF), preferred_element_type=F32)
    pack(row_send.at[0], o[0:64], m, l)
    pack(row_send.at[1], o[64:128], m, l)
    side_send[...] = jnp.concatenate(
        [res_v[...], jnp.broadcast_to(gain_v[...].astype(F32).reshape(1, 64), (8, 64)).astype(BF)], axis=1
    )

    pl.semaphore_wait(barrier, len(PLANE) + len(DEPTH))

    def send(src, dst, sends, recvs, device):
        pltpu.make_async_remote_copy(src, dst, sends, recvs, device_id=device, device_id_type=MESH).start()

    def whole(ref, sem):
        pltpu.make_async_copy(ref, ref, sem).wait()

    for j, o_ in enumerate(ROW):
        send(row_send.at[cs[o_[2]]], row_recv.at[j], send_sem.at[0], recv_sem.at[0], (index(o_), z))
    for j, dz in enumerate(DEPTH):
        send(side_send, side_recv.at[j], send_sem.at[1], recv_sem.at[1], (kvp, zs[dz]))
    whole(row_recv, recv_sem.at[0])
    o, m, l = combine([unpack(row_send[c])] + [unpack(row_recv[j]) for j in range(len(ROW))])
    pack(col_send, o, m, l)

    for j, o_ in enumerate(COL):
        send(col_send, col_recv.at[j], send_sem.at[2], recv_sem.at[2], (index(o_), z))
    whole(side_recv, recv_sem.at[1])
    lane8 = lax.broadcasted_iota(jnp.int32, (8, 128), 1)
    low = lane8 < 64
    side = [side_send[...].astype(F32)] + [side_recv[j].astype(F32) for j in range(Z - 1)]
    owner = [z] + [zs[Z - dz] for dz in DEPTH]
    res_parts, gain_parts = [], []
    for g in range(Z // 2):
        r, gn = jnp.zeros((8, 128), F32), jnp.zeros((8, 128), F32)
        for t, own in zip(side, owner):
            turned = pltpu.roll(t, 64, 1)
            here = (jnp.zeros((8, 128), jnp.int32) + own) == jnp.where(low, 2 * g, 2 * g + 1)
            r = jnp.where(here, jnp.where(low, t, turned), r)
            gn = jnp.where(here, jnp.where(low, turned, t), gn)
        res_parts.append(r)
        gain_parts.append(gn)
    res = jnp.concatenate(res_parts, axis=1)
    gain = jnp.concatenate(gain_parts, axis=1)
    whole(col_recv, recv_sem.at[2])
    own = [unpack(col_send[...])] + [unpack(col_recv[j]) for j, o_ in enumerate(COL) if o_[2] == 0]
    other = [unpack(col_recv[j]) for j, o_ in enumerate(COL) if o_[2] == 1]
    o, _, l = combine(own)
    own = o / l
    o, _, l = combine(other)
    other = o / l
    first = (jnp.zeros((64, 128), jnp.int32) + c) == 0
    att = jnp.concatenate([jnp.where(first, own, other), jnp.where(first, other, own)], axis=0).T
    att = jnp.concatenate([att[8 * h : 8 * h + 8] for h in range(16)], axis=1).astype(BF)

    large[0].wait()
    part = jnp.dot(att, ow_v[...], preferred_element_type=F32)
    proj_send[...] = part.astype(BF)
    for j, dz in enumerate(DEPTH):
        send(proj_send, proj_recv.at[j], send_sem.at[3], recv_sem.at[3], (kvp, zs[dz]))
    whole(proj_recv, recv_sem.at[3])
    total = part
    for j in range(Z - 1):
        total = total + proj_recv[j].astype(F32)
    hidden = (res + total).astype(BF).astype(F32)
    square = jnp.sum(hidden * hidden, axis=1, keepdims=True)
    high = square.astype(BF).astype(F32)
    norm_send[:, pl.ds(0, 512)] = (hidden * gain).astype(BF)
    norm_send[:, pl.ds(512, 128)] = jnp.where(low, high, square - high).astype(BF)

    n = len(CHIPS)
    for j, o_ in enumerate(CHIPS):
        send(norm_send, norm_recv.at[j], send_sem.at[4], norm_sem.at[j], (index(o_), z))
    send(norm_send, pass_recv.at[n], send_sem.at[4], norm_sem.at[2 * n], (index((0, 0, 1)), z))
    for copy in large[1:3]:
        copy.wait()

    def gate_up(ref, block, gate, up):
        feats = ref[:, pl.ds(0, 512)]
        cols = pl.ds(pl.multiple_of(block * 512, 512), 512)
        gate = gate + lax.dot_general(feats, gw_v[:, cols], contract, preferred_element_type=F32)
        up = up + lax.dot_general(feats, uw_v[:, cols], contract, preferred_element_type=F32)
        return gate, up, ref[:, pl.ds(512, 128)].astype(F32)

    gate = jnp.zeros((8, 104), F32)
    up = jnp.zeros((8, 104), F32)
    gate, up, squares = gate_up(norm_send, kvp, gate, up)
    lag = 4
    for step in range(n + 1 + lag):
        if step < n:
            j = n - 1 - step
            slot = norm_recv.at[j]
            whole(slot, norm_sem.at[j])
            send(slot, pass_recv.at[j], send_sem.at[4], norm_sem.at[n + j], (index((0, 0, 1)), z))
            gate, up, extra = gate_up(slot, origin(CHIPS[j]), gate, up)
            squares = squares + extra
        if step >= lag:
            j = n - (step - lag)
            slot = pass_recv.at[j]
            whole(slot, norm_sem.at[n + j])
            o_ = CHIPS[j] if j < n else (0, 0, 0)
            gate, up, extra = gate_up(slot, origin((o_[0], o_[1], 1)), gate, up)
            squares = squares + extra
    squares = squares[:, 0:1] + squares[:, 64:65]
    inverse = lax.rsqrt(squares * (1.0 / D) + EPS)
    gate = gate * inverse
    up = up * inverse
    inner = (gate / (1.0 + jnp.exp(-gate)) * up).astype(BF)

    large[3].wait()

    def down(block):
        cols = pl.ds(pl.multiple_of(block * 512, 512), 512)
        return jnp.dot(inner, dw_v[:, cols], preferred_element_type=F32)

    order = CHIPS + [(0, 0, 0)]
    sibling = (index((0, 0, 1)), z)
    for g in range(len(order) // GROUP):
        for j in range(GROUP * g, GROUP * g + GROUP):
            pair_send[j] = down(index((order[j][0], order[j][1], 1))).astype(BF)
        slots = pl.ds(GROUP * g, GROUP)
        send(pair_send.at[slots], pair_recv.at[slots], send_sem.at[5], pair_sem.at[g], sibling)
    for g in range(len(order) // GROUP):
        js = range(GROUP * g, GROUP * g + GROUP)
        blocks = [down(index(order[j])) for j in js]
        whole(pair_recv.at[pl.ds(GROUP * g, GROUP)], pair_sem.at[g])
        for j, block in zip(js, blocks):
            total = block + pair_recv[j].astype(F32)
            if j < n:
                down_send[j] = total.astype(BF)
                send(down_send.at[j], down_recv.at[j], send_sem.at[7], recv_sem.at[4], (index(order[j]), z))
    whole(down_recv, recv_sem.at[4])
    for j in range(n):
        total = total + down_recv[j].astype(F32)

    for g in range(Z // 2):
        last_send[g] = total[:, 128 * g : 128 * g + 128]
    for j, dz in enumerate(DEPTH):
        send(last_send.at[zs[dz] // 2], last_recv.at[j], send_sem.at[6], recv_sem.at[5], (kvp, zs[dz]))
    mine = last_send[z // 2]
    hid = jnp.zeros((8, 128), F32)
    for g in range(Z // 2):
        hid = jnp.where((jnp.zeros((8, 128), jnp.int32) + z // 2) == g, hidden[:, 128 * g : 128 * g + 128], hid)
    whole(last_recv, recv_sem.at[5])
    for j in range(Z - 1):
        mine = mine + last_recv[j]
    mine = mine + hid
    odd = (jnp.zeros((8, 128), jnp.int32) + lax.rem(z, 2)) == 1
    mine = jnp.where(odd, pltpu.roll(mine, 64, 1), mine)
    out_ref[...] = mine[:, 0:64].astype(BF)

    for i, ref in enumerate((row_recv, side_recv, col_recv, proj_recv, norm_recv, pair_recv, last_recv, down_recv)):
        whole(ref, send_sem.at[i])
    whole(pass_recv, send_sem.at[4])


def local(residual, norm_gain, queries, keys, values, new_kv, lens, out_weight, gate_weight, up_weight, down_weight):
    V = pltpu.VMEM
    n = len(CHIPS)
    scratch = [
        V((8, 64), BF), V((64,), BF), V((8, 16, 128), BF), V((8, 128, 128), BF), V((8, 128, 128), BF),
        V((8, 2, 128), BF), pltpu.SMEM((8,), jnp.int32), V((2048, 512), BF),
        V((104, D), BF), V((104, D), BF), V((104, D), BF),
        V((2, 80, 128), BF), V((7, 80, 128), BF), V((80, 128), BF), V((7, 80, 128), BF),
        V((8, 128), BF), V((7, 8, 128), BF),
        V((8, 512), BF), V((7, 8, 512), BF), V((8, 640), BF), V((n, 8, 640), BF), V((n + 1, 8, 640), BF),
        V((n + 1, 8, 512), BF), V((n + 1, 8, 512), BF),
        V((n, 8, 512), BF), V((n, 8, 512), BF), V((4, 8, 128), F32), V((7, 8, 128), F32),
        pltpu.SemaphoreType.DMA((11,)), pltpu.SemaphoreType.DMA((8,)), pltpu.SemaphoreType.DMA((6,)),
        pltpu.SemaphoreType.DMA((2 * n + 1,)), pltpu.SemaphoreType.DMA(((n + 1) // GROUP,)),
    ]
    return pl.pallas_call(
        kernel,
        name="decode_step",
        out_shape=jax.ShapeDtypeStruct((8, 64), BF),
        in_specs=[pl.BlockSpec(memory_space=pltpu.HBM)] * 11,
        out_specs=pl.BlockSpec(memory_space=pltpu.VMEM),
        scratch_shapes=scratch,
        cost_estimate=pl.CostEstimate(flops=120_000_000, bytes_accessed=13_000_000, transcendentals=20_000),
        compiler_params=pltpu.CompilerParams(collective_id=0, has_side_effects=True, vmem_limit_bytes=60 << 20),
    )(
        residual, norm_gain, queries, keys.reshape(8, 128, 128), values.reshape(8, 128, 128),
        new_kv.reshape(8, 2, 128), lens, out_weight, gate_weight, up_weight, down_weight,
    )


def solution(mesh):
    in_specs = (
        P(None, ("kvp", "tp")),
        P(("kvp", "tp")),
        P(None, "tp", None),
        P(None, "kvp", "tp", None),
        P(None, "kvp", "tp", None),
        P(None, None, "tp", None),
        P(),
        P("tp", "kvp"),
        P(("kvp", "tp"), None),
        P(("kvp", "tp"), None),
        P(("kvp", "tp"), None),
    )
    out_specs = P(None, ("kvp", "tp"))
    return jax.shard_map(local, mesh=mesh, in_specs=in_specs, out_specs=out_specs, check_vma=False)
```

```python
import functools
import math

import jax
import jax.numpy as jnp
from jax import lax
from jax.experimental import pallas as pl
from jax.experimental.pallas import tpu as pltpu
from jax.sharding import PartitionSpec as P

MESH = pl.DeviceIdType.MESH
BF = jnp.bfloat16
F32 = jnp.float32
D = 16384
EPS = 1e-05
EMPTY = -1e30
X, Y, C, Z = 4, 4, 2, 8
KVP = X * Y * C


def hops(dx, dy):
    return min(dx, X - dx) + min(dy, Y - dy)


ROW = sorted([(dx, 0, dc) for dx in range(X) for dc in range(C)][1:], key=lambda o: -hops(o[0], o[1]))
COL = sorted([(0, dy, dc) for dy in range(Y) for dc in range(C)][1:], key=lambda o: -hops(o[0], o[1]))
PLANE = sorted(
    [(dx, dy, dc) for dx in range(X) for dy in range(Y) for dc in range(C)][1:],
    key=lambda o: (-hops(o[0], o[1]), -o[2]),
)
NEAR = [o for o in PLANE if o[2] == 0 and hops(o[0], o[1]) <= 2]
FAR = [o for o in PLANE if hops(o[0], o[1]) > 2]
NEAR_SPANS = [(0, 6), (6, 10)]
FAR_SPANS = [(0, 2), (2, 10)]
GROUP = 4
CHIPS = [o for o in PLANE if o[2] == 0]
DEPTH = sorted(range(1, Z), key=lambda dz: -min(dz, Z - dz))
GREET = [(dx, 0, dc, 0) for dx in range(X) for dc in range(C)] + [(0, dy, dc, 0) for dy in range(1, Y) for dc in range(C)]
GREET = GREET[1:] + [(0, 0, 0, dz) for dz in (1, 2, Z - 2, Z - 1)]
GREET = sorted(GREET, key=lambda o: -hops(o[0], o[1]) - min(o[3], Z - o[3]))


def pack(ref, o, m, l):
    rows = lax.broadcasted_iota(jnp.int32, (16, 128), 0)
    high = l.astype(BF).astype(F32)
    tail = jnp.where(rows == 0, m, jnp.where(rows == 1, high, jnp.where(rows == 2, l - high, 0.0)))
    ref[pl.ds(0, 64), :] = o.astype(BF)
    ref[pl.ds(64, 16), :] = tail.astype(BF)


def unpack(x):
    o = x[0:64].astype(F32)
    tail = x[64:80].astype(F32)
    return o, tail[0:1], tail[1:2] + tail[2:3]


def combine(parts):
    m = functools.reduce(jnp.maximum, [p[1] for p in parts])
    o, l = 0.0, 0.0
    for po, pm, pl_ in parts:
        factor = jnp.exp(pm - m)
        o = o + po * factor
        l = l + pl_ * factor
    return o, m, l


def kernel(
    res_h, gain_h, q_h, k_h, v_h, nkv_h, lens_h, ow_h, gw_h, uw_h, dw_h,
    out_ref,
    res_v, gain_v, q_v, k_v, v_v, nkv_v, lens_s, ow_v, gw_v, uw_v, dw_v,
    row_send, row_recv, col_send, col_recv, side_send, side_recv,
    proj_send, proj_recv, norm_send, norm_recv, pass_recv, far_recv, pair_send, pair_recv, down_send, down_recv, last_send, last_recv,
    load_sem, send_sem, recv_sem, norm_sem, pair_sem, side_sem,
):
    kvp = lax.axis_index("kvp")
    z = lax.axis_index("tp")
    x = kvp // (Y * C)
    y = lax.rem(kvp // C, Y)
    c = lax.rem(kvp, C)
    xs = [x] + [lax.rem(x + d, X) for d in range(1, X)]
    ys = [y] + [lax.rem(y + d, Y) for d in range(1, Y)]
    cs = [c, 1 - c]
    zs = [z] + [lax.rem(z + d, Z) for d in range(1, Z)]

    def index(o):
        return (xs[o[0]] * Y + ys[o[1]]) * C + cs[o[2]]

    def origin(o):
        return index(((X - o[0]) % X, (Y - o[1]) % Y, (C - o[2]) % C))

    small = [(k_h, k_v), (q_h, q_v), (v_h, v_v), (nkv_h, nkv_v), (lens_h, lens_s), (res_h, res_v), (gain_h, gain_v)]
    large = [(ow_h, ow_v), (gw_h, gw_v), (uw_h, uw_v), (dw_h, dw_v)]
    small = [pltpu.make_async_copy(s, d, load_sem.at[i]) for i, (s, d) in enumerate(small)]
    large = [pltpu.make_async_copy(s, d, load_sem.at[7 + i]) for i, (s, d) in enumerate(large)]
    for copy in small:
        copy.start()

    barrier = pltpu.get_barrier_semaphore()
    for o in GREET:
        pl.semaphore_signal(barrier, inc=1, device_id=(index(o), zs[o[3]]), device_id_type=MESH)

    for copy in small:
        copy.wait()
    for copy in large:
        copy.start()

    scale = 1.0 / math.sqrt(128)
    ri = lax.broadcasted_iota(jnp.int32, (128, 128), 0)
    li = lax.broadcasted_iota(jnp.int32, (128, 128), 1)
    perm = (li == (ri & 7) * 16 + (ri >> 3)).astype(BF)
    q = jnp.dot(perm, q_v[...].reshape(128, 128), preferred_element_type=F32)
    qm = jnp.concatenate([jnp.where((ri & 7) == b, q, 0.0).astype(BF) for b in range(8)], axis=1)
    kc = jnp.concatenate([k_v[b] for b in range(8)], axis=1)
    nkv = nkv_v[...].astype(F32)
    nk = nkv[:, 0, :]
    nv = nkv[:, 1, :]
    nkc = jnp.concatenate([jnp.broadcast_to(nk[b : b + 1], (8, 128)) for b in range(8)], axis=1).astype(BF)
    contract = (((1,), (1,)), ((), ()))
    s = lax.dot_general(kc, qm, contract, preferred_element_type=F32) * scale
    fresh = lax.dot_general(nkc, qm, contract, preferred_element_type=F32)[0:1] * scale
    lane = lax.broadcasted_iota(jnp.int32, (1, 128), 1) & 7
    limit = functools.reduce(lambda a, b: jnp.where(lane == b, lens_s[b], a), range(1, 8), jnp.full((1, 128), lens_s[0]))
    live = (ri + kvp * 128) < limit
    mine = (jnp.zeros((1, 128), jnp.int32) + kvp) == 0
    s = jnp.where(live, s, EMPTY)
    fresh = jnp.where(mine, fresh, EMPTY)
    m = jnp.maximum(jnp.max(s, axis=0, keepdims=True), fresh)
    m = m.astype(BF).astype(F32)
    p = jnp.where(live, jnp.exp(s - m), 0.0)
    pf = jnp.where(mine, jnp.exp(fresh - m), 0.0)
    l = jnp.sum(p, axis=0, keepdims=True) + pf
    pm = jnp.concatenate([jnp.where((li & 7) == b, p, 0.0).astype(BF) for b in range(8)], axis=0)
    vt = jnp.concatenate([v_v[b].T for b in range(8)], axis=1)
    o = jnp.dot(vt, pm, preferred_element_type=F32)
    ri8 = lax.broadcasted_iota(jnp.int32, (8, 128), 0)
    li8 = lax.broadcasted_iota(jnp.int32, (8, 128), 1)
    pfm = jnp.where((li8 & 7) == ri8, pf, 0.0)
    pad = jnp.zeros((120, 128), F32)
    nvt = jnp.concatenate([nv, pad], axis=0).T.astype(BF)
    o = o + jnp.dot(nvt, jnp.concatenate([pfm, pad], axis=0).astype(BF), preferred_element_type=F32)
    pack(row_send.at[0], o[0:64], m, l)
    pack(row_send.at[1], o[64:128], m, l)
    side_send[...] = jnp.concatenate(
        [res_v[...], jnp.broadcast_to(gain_v[...].astype(F32).reshape(1, 64), (8, 64)).astype(BF)], axis=1
    )

    pl.semaphore_wait(barrier, len(GREET))

    def send(src, dst, sends, recvs, device):
        pltpu.make_async_remote_copy(src, dst, sends, recvs, device_id=device, device_id_type=MESH).start()

    def whole(ref, sem):
        pltpu.make_async_copy(ref, ref, sem).wait()

    for j, o_ in enumerate(ROW):
        send(row_send.at[cs[o_[2]]], row_recv.at[j], send_sem.at[0], recv_sem.at[0], (index(o_), z))
    for j, dz in enumerate(DEPTH):
        if min(dz, Z - dz) <= 2:
            send(side_send, side_recv.at[j], send_sem.at[1], side_sem.at[j], (kvp, zs[dz]))
    whole(row_recv, recv_sem.at[0])
    o, m, l = combine([unpack(row_send[c])] + [unpack(row_recv[j]) for j in range(len(ROW))])
    pack(col_send, o, m, l)

    for j, o_ in enumerate(COL):
        send(col_send, col_recv.at[j], send_sem.at[2], recv_sem.at[2], (index(o_), z))
    for j, dz in enumerate(DEPTH):
        if min(dz, Z - dz) <= 2:
            whole(side_recv.at[j], side_sem.at[j])
    for j, dz in enumerate(DEPTH):
        if min(dz, Z - dz) > 2:
            send(side_send, side_recv.at[j], send_sem.at[1], side_sem.at[j], (kvp, zs[dz]))
    for j, dz in enumerate(DEPTH):
        if min(dz, Z - dz) > 2:
            whole(side_recv.at[j], side_sem.at[j])
    lane8 = lax.broadcasted_iota(jnp.int32, (8, 128), 1)
    low = lane8 < 64
    side = [side_send[...].astype(F32)] + [side_recv[j].astype(F32) for j in range(Z - 1)]
    owner = [z] + [zs[Z - dz] for dz in DEPTH]
    res_parts, gain_parts = [], []
    for g in range(Z // 2):
        r, gn = jnp.zeros((8, 128), F32), jnp.zeros((8, 128), F32)
        for t, own in zip(side, owner):
            turned = pltpu.roll(t, 64, 1)
            here = (jnp.zeros((8, 128), jnp.int32) + own) == jnp.where(low, 2 * g, 2 * g + 1)
            r = jnp.where(here, jnp.where(low, t, turned), r)
            gn = jnp.where(here, jnp.where(low, turned, t), gn)
        res_parts.append(r)
        gain_parts.append(gn)
    res = jnp.concatenate(res_parts, axis=1)
    gain = jnp.concatenate(gain_parts, axis=1)
    whole(col_recv, recv_sem.at[2])
    own = [unpack(col_send[...])] + [unpack(col_recv[j]) for j, o_ in enumerate(COL) if o_[2] == 0]
    other = [unpack(col_recv[j]) for j, o_ in enumerate(COL) if o_[2] == 1]
    o, _, l = combine(own)
    own = o / l
    o, _, l = combine(other)
    other = o / l
    first = (jnp.zeros((64, 128), jnp.int32) + c) == 0
    att = jnp.concatenate([jnp.where(first, own, other), jnp.where(first, other, own)], axis=0).T
    att = jnp.concatenate([att[8 * h : 8 * h + 8] for h in range(16)], axis=1).astype(BF)

    large[0].wait()
    part = jnp.dot(att, ow_v[...], preferred_element_type=F32)
    proj_send[...] = part.astype(BF)
    for j, dz in enumerate(DEPTH):
        send(proj_send, proj_recv.at[j], send_sem.at[3], recv_sem.at[3], (kvp, zs[dz]))
    whole(proj_recv, recv_sem.at[3])
    total = part
    for j in range(Z - 1):
        total = total + proj_recv[j].astype(F32)
    hidden = (res + total).astype(BF).astype(F32)
    square = jnp.sum(hidden * hidden, axis=1, keepdims=True)
    high = square.astype(BF).astype(F32)
    norm_send[:, pl.ds(0, 512)] = (hidden * gain).astype(BF)
    norm_send[:, pl.ds(512, 128)] = jnp.where(low, high, square - high).astype(BF)

    n = len(NEAR)
    sibling = (index((0, 0, 1)), z)
    span_of = lambda spans, j: max(k for k, (lo, _) in enumerate(spans) if lo <= j)
    for j, o_ in enumerate(NEAR):
        send(norm_send, norm_recv.at[j], send_sem.at[4], norm_sem.at[span_of(NEAR_SPANS, j)], (index(o_), z))
    for j, o_ in enumerate(FAR):
        send(norm_send, far_recv.at[j], send_sem.at[8], norm_sem.at[2 + span_of(FAR_SPANS, j)], (index(o_), z))
    send(norm_send, pass_recv.at[n], send_sem.at[4], norm_sem.at[4], sibling)
    for copy in large[1:3]:
        copy.wait()

    def gate_up(ref, block, gate, up):
        feats = ref[:, pl.ds(0, 512)]
        cols = pl.ds(pl.multiple_of(block * 512, 512), 512)
        gate = gate + lax.dot_general(feats, gw_v[:, cols], contract, preferred_element_type=F32)
        up = up + lax.dot_general(feats, uw_v[:, cols], contract, preferred_element_type=F32)
        return gate, up, ref[:, pl.ds(512, 128)].astype(F32)

    gate = jnp.zeros((8, 104), F32)
    up = jnp.zeros((8, 104), F32)
    gate, up, squares = gate_up(norm_send, kvp, gate, up)
    for k, (lo, hi) in reversed(list(enumerate(NEAR_SPANS))):
        slots = norm_recv.at[pl.ds(lo, hi - lo)]
        whole(slots, norm_sem.at[k])
        send(slots, pass_recv.at[pl.ds(lo, hi - lo)], send_sem.at[4], norm_sem.at[5 + k], sibling)
        for j in reversed(range(lo, hi)):
            gate, up, extra = gate_up(norm_recv.at[j], origin(NEAR[j]), gate, up)
            squares = squares + extra
    whole(pass_recv.at[n], norm_sem.at[4])
    gate, up, extra = gate_up(pass_recv.at[n], origin((0, 0, 1)), gate, up)
    squares = squares + extra
    for k, (lo, hi) in reversed(list(enumerate(NEAR_SPANS))):
        whole(pass_recv.at[pl.ds(lo, hi - lo)], norm_sem.at[5 + k])
        for j in reversed(range(lo, hi)):
            gate, up, extra = gate_up(pass_recv.at[j], origin((NEAR[j][0], NEAR[j][1], 1)), gate, up)
            squares = squares + extra
    for k, (lo, hi) in reversed(list(enumerate(FAR_SPANS))):
        whole(far_recv.at[pl.ds(lo, hi - lo)], norm_sem.at[2 + k])
        for j in reversed(range(lo, hi)):
            gate, up, extra = gate_up(far_recv.at[j], origin(FAR[j]), gate, up)
            squares = squares + extra
    squares = squares[:, 0:1] + squares[:, 64:65]
    inverse = lax.rsqrt(squares * (1.0 / D) + EPS)
    gate = gate * inverse
    up = up * inverse
    inner = (gate / (1.0 + jnp.exp(-gate)) * up).astype(BF)

    large[3].wait()

    def down(block):
        cols = pl.ds(pl.multiple_of(block * 512, 512), 512)
        return jnp.dot(inner, dw_v[:, cols], preferred_element_type=F32)

    n = len(CHIPS)
    order = CHIPS + [(0, 0, 0)]
    sibling = (index((0, 0, 1)), z)
    for g in range(len(order) // GROUP):
        for j in range(GROUP * g, GROUP * g + GROUP):
            pair_send[j] = down(index((order[j][0], order[j][1], 1))).astype(BF)
        slots = pl.ds(GROUP * g, GROUP)
        send(pair_send.at[slots], pair_recv.at[slots], send_sem.at[5], pair_sem.at[g], sibling)
    for g in range(len(order) // GROUP):
        js = range(GROUP * g, GROUP * g + GROUP)
        blocks = [down(index(order[j])) for j in js]
        whole(pair_recv.at[pl.ds(GROUP * g, GROUP)], pair_sem.at[g])
        for j, block in zip(js, blocks):
            total = block + pair_recv[j].astype(F32)
            if j < n:
                down_send[j] = total.astype(BF)
                send(down_send.at[j], down_recv.at[j], send_sem.at[7], recv_sem.at[4], (index(order[j]), z))
    whole(down_recv, recv_sem.at[4])
    for j in range(n):
        total = total + down_recv[j].astype(F32)

    for g in range(Z // 2):
        last_send[g] = total[:, 128 * g : 128 * g + 128]
    for j, dz in enumerate(DEPTH):
        send(last_send.at[zs[dz] // 2], last_recv.at[j], send_sem.at[6], recv_sem.at[5], (kvp, zs[dz]))
    mine = last_send[z // 2]
    hid = jnp.zeros((8, 128), F32)
    for g in range(Z // 2):
        hid = jnp.where((jnp.zeros((8, 128), jnp.int32) + z // 2) == g, hidden[:, 128 * g : 128 * g + 128], hid)
    whole(last_recv, recv_sem.at[5])
    for j in range(Z - 1):
        mine = mine + last_recv[j]
    mine = mine + hid
    odd = (jnp.zeros((8, 128), jnp.int32) + lax.rem(z, 2)) == 1
    mine = jnp.where(odd, pltpu.roll(mine, 64, 1), mine)
    out_ref[...] = mine[:, 0:64].astype(BF)

    for i, ref in enumerate((row_recv, side_recv, col_recv, proj_recv, norm_recv, pair_recv, last_recv, down_recv, far_recv)):
        whole(ref, send_sem.at[i])
    whole(pass_recv, send_sem.at[4])


def local(residual, norm_gain, queries, keys, values, new_kv, lens, out_weight, gate_weight, up_weight, down_weight):
    V = pltpu.VMEM
    n, far = len(NEAR), len(FAR)
    scratch = [
        V((8, 64), BF), V((64,), BF), V((8, 16, 128), BF), V((8, 128, 128), BF), V((8, 128, 128), BF),
        V((8, 2, 128), BF), pltpu.SMEM((8,), jnp.int32), V((2048, 512), BF),
        V((104, D), BF), V((104, D), BF), V((104, D), BF),
        V((2, 80, 128), BF), V((7, 80, 128), BF), V((80, 128), BF), V((7, 80, 128), BF),
        V((8, 128), BF), V((7, 8, 128), BF),
        V((8, 512), BF), V((7, 8, 512), BF),
        V((8, 640), BF), V((n, 8, 640), BF), V((n + 1, 8, 640), BF), V((far, 8, 640), BF),
        V((16, 8, 512), BF), V((16, 8, 512), BF),
        V((len(CHIPS), 8, 512), BF), V((len(CHIPS), 8, 512), BF), V((4, 8, 128), F32), V((7, 8, 128), F32),
        pltpu.SemaphoreType.DMA((11,)), pltpu.SemaphoreType.DMA((9,)), pltpu.SemaphoreType.DMA((6,)),
        pltpu.SemaphoreType.DMA((7,)), pltpu.SemaphoreType.DMA((4,)), pltpu.SemaphoreType.DMA((Z - 1,)),
    ]
    return pl.pallas_call(
        kernel,
        name="decode_step",
        out_shape=jax.ShapeDtypeStruct((8, 64), BF),
        in_specs=[pl.BlockSpec(memory_space=pltpu.HBM)] * 11,
        out_specs=pl.BlockSpec(memory_space=pltpu.VMEM),
        scratch_shapes=scratch,
        cost_estimate=pl.CostEstimate(flops=120_000_000, bytes_accessed=13_000_000, transcendentals=20_000),
        compiler_params=pltpu.CompilerParams(collective_id=0, has_side_effects=True, vmem_limit_bytes=60 << 20),
    )(
        residual, norm_gain, queries, keys.reshape(8, 128, 128), values.reshape(8, 128, 128),
        new_kv.reshape(8, 2, 128), lens, out_weight, gate_weight, up_weight, down_weight,
    )


def solution(mesh):
    in_specs = (
        P(None, ("kvp", "tp")),
        P(("kvp", "tp")),
        P(None, "tp", None),
        P(None, "kvp", "tp", None),
        P(None, "kvp", "tp", None),
        P(None, None, "tp", None),
        P(),
        P("tp", "kvp"),
        P(("kvp", "tp"), None),
        P(("kvp", "tp"), None),
        P(("kvp", "tp"), None),
    )
    out_specs = P(None, ("kvp", "tp"))
    return jax.shard_map(local, mesh=mesh, in_specs=in_specs, out_specs=out_specs, check_vma=False)
```

```python
import functools
import math

import jax
import jax.numpy as jnp
from jax import lax
from jax.experimental import pallas as pl
from jax.experimental.pallas import tpu as pltpu
from jax.sharding import PartitionSpec as P

MESH = pl.DeviceIdType.MESH
BF = jnp.bfloat16
F32 = jnp.float32
D = 16384
EPS = 1e-05
EMPTY = -1e30
X, Y, C, Z = 4, 4, 2, 8
KVP = X * Y * C


def hops(dx, dy):
    return min(dx, X - dx) + min(dy, Y - dy)


ROW = sorted([(dx, 0, dc) for dx in range(X) for dc in range(C)][1:], key=lambda o: -hops(o[0], o[1]))
COL = sorted([(0, dy, dc) for dy in range(Y) for dc in range(C)][1:], key=lambda o: -hops(o[0], o[1]))
PLANE = sorted(
    [(dx, dy, dc) for dx in range(X) for dy in range(Y) for dc in range(C)][1:],
    key=lambda o: (-hops(o[0], o[1]), -o[2]),
)
NEAR = [o for o in PLANE if o[2] == 0 and hops(o[0], o[1]) <= 2]
FAR = [o for o in PLANE if hops(o[0], o[1]) > 2]
NEAR_SPANS = [(0, 6), (6, 10)]
FAR_SPANS = [(0, 2), (2, 10)]
GROUP = 4
CHIPS = [o for o in PLANE if o[2] == 0]
DEPTH = sorted(range(1, Z), key=lambda dz: -min(dz, Z - dz))
GREET = [(dx, 0, dc, 0) for dx in range(X) for dc in range(C)] + [(0, dy, dc, 0) for dy in range(1, Y) for dc in range(C)]
GREET = GREET[1:] + [(0, 0, 0, dz) for dz in (1, 2, Z - 2, Z - 1)]
GREET = sorted(GREET, key=lambda o: -hops(o[0], o[1]) - min(o[3], Z - o[3]))


def pack(ref, o, m, l):
    rows = lax.broadcasted_iota(jnp.int32, (8, 128), 0)
    high = l.astype(BF).astype(F32)
    tail = jnp.where(rows == 0, m, jnp.where(rows == 1, high, jnp.where(rows == 2, l - high, 0.0)))
    ref[pl.ds(0, 8)] = o.reshape(8, 8, 128).astype(BF)
    ref[8] = tail.astype(BF)


def unpack(x):
    o = x[0:8].astype(F32).reshape(64, 128)
    tail = x[8].astype(F32)
    return o, tail[0:1], tail[1:2] + tail[2:3]


def combine(parts):
    m = functools.reduce(jnp.maximum, [p[1] for p in parts])
    o, l = 0.0, 0.0
    for po, pm, pl_ in parts:
        factor = jnp.exp(pm - m)
        o = o + po * factor
        l = l + pl_ * factor
    return o, m, l


def kernel(
    res_h, gain_h, q_h, k_h, v_h, nkv_h, lens_h, ow_h, gw_h, uw_h, dw_h,
    out_ref,
    res_v, gain_v, q_v, k_v, v_v, nkv_v, lens_s, ow_v, gw_v, uw_v, dw_v,
    row_send, row_recv, col_send, col_recv, side_send, side_recv,
    proj_send, proj_recv, norm_send, norm_recv, pass_recv, far_recv, pair_send, pair_recv, down_send, down_recv, last_send, last_recv,
    load_sem, send_sem, recv_sem, norm_sem, pair_sem, side_sem,
):
    kvp = lax.axis_index("kvp")
    z = lax.axis_index("tp")
    x = kvp // (Y * C)
    y = lax.rem(kvp // C, Y)
    c = lax.rem(kvp, C)
    xs = [x] + [lax.rem(x + d, X) for d in range(1, X)]
    ys = [y] + [lax.rem(y + d, Y) for d in range(1, Y)]
    cs = [c, 1 - c]
    zs = [z] + [lax.rem(z + d, Z) for d in range(1, Z)]

    def index(o):
        return (xs[o[0]] * Y + ys[o[1]]) * C + cs[o[2]]

    def origin(o):
        return index(((X - o[0]) % X, (Y - o[1]) % Y, (C - o[2]) % C))

    small = [(k_h, k_v), (q_h, q_v), (v_h, v_v), (nkv_h, nkv_v), (lens_h, lens_s), (res_h, res_v), (gain_h, gain_v)]
    large = [(ow_h, ow_v), (gw_h, gw_v), (uw_h, uw_v), (dw_h, dw_v)]
    small = [pltpu.make_async_copy(s, d, load_sem.at[i]) for i, (s, d) in enumerate(small)]
    large = [pltpu.make_async_copy(s, d, load_sem.at[7 + i]) for i, (s, d) in enumerate(large)]
    for copy in small:
        copy.start()

    barrier = pltpu.get_barrier_semaphore()
    for o in GREET:
        pl.semaphore_signal(barrier, inc=1, device_id=(index(o), zs[o[3]]), device_id_type=MESH)

    for copy in small:
        copy.wait()
    for copy in large:
        copy.start()

    scale = 1.0 / math.sqrt(128)
    ri = lax.broadcasted_iota(jnp.int32, (128, 128), 0)
    li = lax.broadcasted_iota(jnp.int32, (128, 128), 1)
    perm = (li == (ri & 7) * 16 + (ri >> 3)).astype(BF)
    q = jnp.dot(perm, q_v[...].reshape(128, 128), preferred_element_type=F32)
    qm = jnp.concatenate([jnp.where((ri & 7) == b, q, 0.0).astype(BF) for b in range(8)], axis=1)
    kc = jnp.concatenate([k_v[b] for b in range(8)], axis=1)
    nkv = nkv_v[...].astype(F32)
    nk = nkv[:, 0, :]
    nv = nkv[:, 1, :]
    nkc = jnp.concatenate([jnp.broadcast_to(nk[b : b + 1], (8, 128)) for b in range(8)], axis=1).astype(BF)
    contract = (((1,), (1,)), ((), ()))
    s = lax.dot_general(kc, qm, contract, preferred_element_type=F32) * scale
    fresh = lax.dot_general(nkc, qm, contract, preferred_element_type=F32)[0:1] * scale
    lane = lax.broadcasted_iota(jnp.int32, (1, 128), 1) & 7
    limit = functools.reduce(lambda a, b: jnp.where(lane == b, lens_s[b], a), range(1, 8), jnp.full((1, 128), lens_s[0]))
    live = (ri + kvp * 128) < limit
    mine = (jnp.zeros((1, 128), jnp.int32) + kvp) == 0
    s = jnp.where(live, s, EMPTY)
    fresh = jnp.where(mine, fresh, EMPTY)
    m = jnp.maximum(jnp.max(s, axis=0, keepdims=True), fresh)
    m = m.astype(BF).astype(F32)
    p = jnp.where(live, jnp.exp(s - m), 0.0)
    pf = jnp.where(mine, jnp.exp(fresh - m), 0.0)
    l = jnp.sum(p, axis=0, keepdims=True) + pf
    pm = jnp.concatenate([jnp.where((li & 7) == b, p, 0.0).astype(BF) for b in range(8)], axis=0)
    vt = jnp.concatenate([v_v[b].T for b in range(8)], axis=1)
    o = jnp.dot(vt, pm, preferred_element_type=F32)
    ri8 = lax.broadcasted_iota(jnp.int32, (8, 128), 0)
    li8 = lax.broadcasted_iota(jnp.int32, (8, 128), 1)
    pfm = jnp.where((li8 & 7) == ri8, pf, 0.0)
    pad = jnp.zeros((120, 128), F32)
    nvt = jnp.concatenate([nv, pad], axis=0).T.astype(BF)
    o = o + jnp.dot(nvt, jnp.concatenate([pfm, pad], axis=0).astype(BF), preferred_element_type=F32)
    pack(row_send.at[0], o[0:64], m, l)
    pack(row_send.at[1], o[64:128], m, l)
    side_send[...] = jnp.concatenate(
        [res_v[...], jnp.broadcast_to(gain_v[...].astype(F32).reshape(1, 64), (8, 64)).astype(BF)], axis=1
    )

    pl.semaphore_wait(barrier, len(GREET))

    def send(src, dst, sends, recvs, device):
        pltpu.make_async_remote_copy(src, dst, sends, recvs, device_id=device, device_id_type=MESH).start()

    def whole(ref, sem):
        pltpu.make_async_copy(ref, ref, sem).wait()

    for j, o_ in enumerate(ROW):
        send(row_send.at[cs[o_[2]]], row_recv.at[j], send_sem.at[0], recv_sem.at[0], (index(o_), z))
    for j, dz in enumerate(DEPTH):
        if min(dz, Z - dz) <= 2:
            send(side_send, side_recv.at[j], send_sem.at[1], side_sem.at[j], (kvp, zs[dz]))
    whole(row_recv, recv_sem.at[0])
    o, m, l = combine([unpack(row_send[c])] + [unpack(row_recv[j]) for j in range(len(ROW))])
    pack(col_send, o, m, l)

    for j, o_ in enumerate(COL):
        send(col_send, col_recv.at[j], send_sem.at[2], recv_sem.at[2], (index(o_), z))
    for j, dz in enumerate(DEPTH):
        if min(dz, Z - dz) <= 2:
            whole(side_recv.at[j], side_sem.at[j])
    for j, dz in enumerate(DEPTH):
        if min(dz, Z - dz) > 2:
            send(side_send, side_recv.at[j], send_sem.at[1], side_sem.at[j], (kvp, zs[dz]))
    for j, dz in enumerate(DEPTH):
        if min(dz, Z - dz) > 2:
            whole(side_recv.at[j], side_sem.at[j])
    lane8 = lax.broadcasted_iota(jnp.int32, (8, 128), 1)
    low = lane8 < 64
    side = [side_send[...].astype(F32)] + [side_recv[j].astype(F32) for j in range(Z - 1)]
    owner = [z] + [zs[Z - dz] for dz in DEPTH]
    res_parts, gain_parts = [], []
    for g in range(Z // 2):
        r, gn = jnp.zeros((8, 128), F32), jnp.zeros((8, 128), F32)
        for t, own in zip(side, owner):
            turned = pltpu.roll(t, 64, 1)
            here = (jnp.zeros((8, 128), jnp.int32) + own) == jnp.where(low, 2 * g, 2 * g + 1)
            r = jnp.where(here, jnp.where(low, t, turned), r)
            gn = jnp.where(here, jnp.where(low, turned, t), gn)
        res_parts.append(r)
        gain_parts.append(gn)
    res = jnp.concatenate(res_parts, axis=1)
    gain = jnp.concatenate(gain_parts, axis=1)
    whole(col_recv, recv_sem.at[2])
    own = [unpack(col_send[...])] + [unpack(col_recv[j]) for j, o_ in enumerate(COL) if o_[2] == 0]
    other = [unpack(col_recv[j]) for j, o_ in enumerate(COL) if o_[2] == 1]
    o, _, l = combine(own)
    own = o / l
    o, _, l = combine(other)
    other = o / l
    first = (jnp.zeros((64, 128), jnp.int32) + c) == 0
    att = jnp.concatenate([jnp.where(first, own, other), jnp.where(first, other, own)], axis=0).T
    att = jnp.concatenate([att[8 * h : 8 * h + 8] for h in range(16)], axis=1).astype(BF)

    large[0].wait()
    part = jnp.dot(att, ow_v[...], preferred_element_type=F32)
    proj_send[...] = part.astype(BF)
    for j, dz in enumerate(DEPTH):
        send(proj_send, proj_recv.at[j], send_sem.at[3], recv_sem.at[3], (kvp, zs[dz]))
    whole(proj_recv, recv_sem.at[3])
    total = part
    for j in range(Z - 1):
        total = total + proj_recv[j].astype(F32)
    hidden = (res + total).astype(BF).astype(F32)
    square = jnp.sum(hidden * hidden, axis=1, keepdims=True)
    high = square.astype(BF).astype(F32)
    norm_send[:, pl.ds(0, 512)] = (hidden * gain).astype(BF)
    norm_send[:, pl.ds(512, 128)] = jnp.where(low, high, square - high).astype(BF)

    n = len(NEAR)
    sibling = (index((0, 0, 1)), z)
    span_of = lambda spans, j: max(k for k, (lo, _) in enumerate(spans) if lo <= j)
    for j, o_ in enumerate(NEAR):
        send(norm_send, norm_recv.at[j], send_sem.at[4], norm_sem.at[span_of(NEAR_SPANS, j)], (index(o_), z))
    for j, o_ in enumerate(FAR):
        send(norm_send, far_recv.at[j], send_sem.at[8], norm_sem.at[2 + span_of(FAR_SPANS, j)], (index(o_), z))
    send(norm_send, pass_recv.at[n], send_sem.at[4], norm_sem.at[4], sibling)
    for copy in large[1:3]:
        copy.wait()

    def gate_up(ref, block, gate, up):
        feats = ref[:, pl.ds(0, 512)]
        cols = pl.ds(pl.multiple_of(block * 512, 512), 512)
        gate = gate + lax.dot_general(feats, gw_v[:, cols], contract, preferred_element_type=F32)
        up = up + lax.dot_general(feats, uw_v[:, cols], contract, preferred_element_type=F32)
        return gate, up, ref[:, pl.ds(512, 128)].astype(F32)

    gate = jnp.zeros((8, 104), F32)
    up = jnp.zeros((8, 104), F32)
    gate, up, squares = gate_up(norm_send, kvp, gate, up)
    for k, (lo, hi) in reversed(list(enumerate(NEAR_SPANS))):
        slots = norm_recv.at[pl.ds(lo, hi - lo)]
        whole(slots, norm_sem.at[k])
        send(slots, pass_recv.at[pl.ds(lo, hi - lo)], send_sem.at[4], norm_sem.at[5 + k], sibling)
        for j in reversed(range(lo, hi)):
            gate, up, extra = gate_up(norm_recv.at[j], origin(NEAR[j]), gate, up)
            squares = squares + extra
    whole(pass_recv.at[n], norm_sem.at[4])
    gate, up, extra = gate_up(pass_recv.at[n], origin((0, 0, 1)), gate, up)
    squares = squares + extra
    for k, (lo, hi) in reversed(list(enumerate(NEAR_SPANS))):
        whole(pass_recv.at[pl.ds(lo, hi - lo)], norm_sem.at[5 + k])
        for j in reversed(range(lo, hi)):
            gate, up, extra = gate_up(pass_recv.at[j], origin((NEAR[j][0], NEAR[j][1], 1)), gate, up)
            squares = squares + extra
    for k, (lo, hi) in reversed(list(enumerate(FAR_SPANS))):
        whole(far_recv.at[pl.ds(lo, hi - lo)], norm_sem.at[2 + k])
        for j in reversed(range(lo, hi)):
            gate, up, extra = gate_up(far_recv.at[j], origin(FAR[j]), gate, up)
            squares = squares + extra
    squares = squares[:, 0:1] + squares[:, 64:65]
    inverse = lax.rsqrt(squares * (1.0 / D) + EPS)
    gate = gate * inverse
    up = up * inverse
    inner = (gate / (1.0 + jnp.exp(-gate)) * up).astype(BF)

    large[3].wait()

    def down(block):
        cols = pl.ds(pl.multiple_of(block * 512, 512), 512)
        return jnp.dot(inner, dw_v[:, cols], preferred_element_type=F32)

    n = len(CHIPS)
    order = CHIPS + [(0, 0, 0)]
    sibling = (index((0, 0, 1)), z)
    for g in range(len(order) // GROUP):
        for j in range(GROUP * g, GROUP * g + GROUP):
            pair_send[j] = down(index((order[j][0], order[j][1], 1))).astype(BF)
        slots = pl.ds(GROUP * g, GROUP)
        send(pair_send.at[slots], pair_recv.at[slots], send_sem.at[5], pair_sem.at[g], sibling)
    for g in range(len(order) // GROUP):
        js = range(GROUP * g, GROUP * g + GROUP)
        blocks = [down(index(order[j])) for j in js]
        whole(pair_recv.at[pl.ds(GROUP * g, GROUP)], pair_sem.at[g])
        for j, block in zip(js, blocks):
            total = block + pair_recv[j].astype(F32)
            if j < n:
                down_send[j] = total.astype(BF)
                send(down_send.at[j], down_recv.at[j], send_sem.at[7], recv_sem.at[4], (index(order[j]), z))
    whole(down_recv, recv_sem.at[4])
    for j in range(n):
        total = total + down_recv[j].astype(F32)

    for g in range(Z // 2):
        last_send[g] = total[:, 128 * g : 128 * g + 128]
    for j, dz in enumerate(DEPTH):
        send(last_send.at[zs[dz] // 2], last_recv.at[j], send_sem.at[6], recv_sem.at[5], (kvp, zs[dz]))
    mine = last_send[z // 2]
    hid = jnp.zeros((8, 128), F32)
    for g in range(Z // 2):
        hid = jnp.where((jnp.zeros((8, 128), jnp.int32) + z // 2) == g, hidden[:, 128 * g : 128 * g + 128], hid)
    whole(last_recv, recv_sem.at[5])
    for j in range(Z - 1):
        mine = mine + last_recv[j]
    mine = mine + hid
    odd = (jnp.zeros((8, 128), jnp.int32) + lax.rem(z, 2)) == 1
    mine = jnp.where(odd, pltpu.roll(mine, 64, 1), mine)
    out_ref[...] = mine[:, 0:64].astype(BF)

    for i, ref in enumerate((row_recv, side_recv, col_recv, proj_recv, norm_recv, pair_recv, last_recv, down_recv, far_recv)):
        whole(ref, send_sem.at[i])
    whole(pass_recv, send_sem.at[4])


def local(residual, norm_gain, queries, keys, values, new_kv, lens, out_weight, gate_weight, up_weight, down_weight):
    V = pltpu.VMEM
    n, far = len(NEAR), len(FAR)
    scratch = [
        V((8, 64), BF), V((64,), BF), V((8, 16, 128), BF), V((8, 128, 128), BF), V((8, 128, 128), BF),
        V((8, 2, 128), BF), pltpu.SMEM((8,), jnp.int32), V((2048, 512), BF),
        V((104, D), BF), V((104, D), BF), V((104, D), BF),
        V((2, 9, 8, 128), BF), V((7, 9, 8, 128), BF), V((9, 8, 128), BF), V((7, 9, 8, 128), BF),
        V((8, 128), BF), V((7, 8, 128), BF),
        V((8, 512), BF), V((7, 8, 512), BF),
        V((8, 640), BF), V((n, 8, 640), BF), V((n + 1, 8, 640), BF), V((far, 8, 640), BF),
        V((16, 8, 512), BF), V((16, 8, 512), BF),
        V((len(CHIPS), 8, 512), BF), V((len(CHIPS), 8, 512), BF), V((4, 8, 128), F32), V((7, 8, 128), F32),
        pltpu.SemaphoreType.DMA((11,)), pltpu.SemaphoreType.DMA((9,)), pltpu.SemaphoreType.DMA((6,)),
        pltpu.SemaphoreType.DMA((7,)), pltpu.SemaphoreType.DMA((4,)), pltpu.SemaphoreType.DMA((Z - 1,)),
    ]
    return pl.pallas_call(
        kernel,
        name="decode_step",
        out_shape=jax.ShapeDtypeStruct((8, 64), BF),
        in_specs=[pl.BlockSpec(memory_space=pltpu.HBM)] * 11,
        out_specs=pl.BlockSpec(memory_space=pltpu.VMEM),
        scratch_shapes=scratch,
        cost_estimate=pl.CostEstimate(flops=120_000_000, bytes_accessed=13_000_000, transcendentals=20_000),
        compiler_params=pltpu.CompilerParams(collective_id=0, has_side_effects=True, vmem_limit_bytes=60 << 20),
    )(
        residual, norm_gain, queries, keys.reshape(8, 128, 128), values.reshape(8, 128, 128),
        new_kv.reshape(8, 2, 128), lens, out_weight, gate_weight, up_weight, down_weight,
    )


def solution(mesh):
    in_specs = (
        P(None, ("kvp", "tp")),
        P(("kvp", "tp")),
        P(None, "tp", None),
        P(None, "kvp", "tp", None),
        P(None, "kvp", "tp", None),
        P(None, None, "tp", None),
        P(),
        P("tp", "kvp"),
        P(("kvp", "tp"), None),
        P(("kvp", "tp"), None),
        P(("kvp", "tp"), None),
    )
    out_specs = P(None, ("kvp", "tp"))
    return jax.shard_map(local, mesh=mesh, in_specs=in_specs, out_specs=out_specs, check_vma=False)
```

```python
import functools
import math

import jax
import jax.numpy as jnp
from jax import lax
from jax.experimental import pallas as pl
from jax.experimental.pallas import tpu as pltpu
from jax.sharding import PartitionSpec as P

MESH = pl.DeviceIdType.MESH
BF = jnp.bfloat16
F32 = jnp.float32
D = 16384
EPS = 1e-05
EMPTY = -1e30
X, Y, C, Z = 4, 4, 2, 8
KVP = X * Y * C


def hops(dx, dy):
    return min(dx, X - dx) + min(dy, Y - dy)


ROW = sorted([(dx, 0, dc) for dx in range(X) for dc in range(C)][1:], key=lambda o: -hops(o[0], o[1]))
COL = sorted([(0, dy, dc) for dy in range(Y) for dc in range(C)][1:], key=lambda o: -hops(o[0], o[1]))
PLANE = sorted(
    [(dx, dy, dc) for dx in range(X) for dy in range(Y) for dc in range(C)][1:],
    key=lambda o: (-hops(o[0], o[1]), -o[2]),
)
NEAR = [o for o in PLANE if o[2] == 0 and hops(o[0], o[1]) <= 2]
FAR = [o for o in PLANE if hops(o[0], o[1]) > 2]
NEAR_SPANS = [(0, 6), (6, 10)]
FAR_SPANS = [(0, 10)]
GROUP = 8
CHIPS = [o for o in PLANE if o[2] == 0]
DEPTH = sorted(range(1, Z), key=lambda dz: -min(dz, Z - dz))
GREET = [(dx, 0, dc, 0) for dx in range(X) for dc in range(C)] + [(0, dy, dc, 0) for dy in range(1, Y) for dc in range(C)]
GREET = GREET[1:] + [(0, 0, 0, dz) for dz in (1, 2, Z - 2, Z - 1)]
GREET = sorted(GREET, key=lambda o: -hops(o[0], o[1]) - min(o[3], Z - o[3]))


def pack(ref, o, m, l):
    rows = lax.broadcasted_iota(jnp.int32, (8, 128), 0)
    high = l.astype(BF).astype(F32)
    tail = jnp.where(rows == 0, m, jnp.where(rows == 1, high, jnp.where(rows == 2, l - high, 0.0)))
    ref[pl.ds(0, 8)] = o.reshape(8, 8, 128).astype(BF)
    ref[8] = tail.astype(BF)


def unpack(x):
    o = x[0:8].astype(F32).reshape(64, 128)
    tail = x[8].astype(F32)
    return o, tail[0:1], tail[1:2] + tail[2:3]


def combine(parts):
    m = functools.reduce(jnp.maximum, [p[1] for p in parts])
    o, l = 0.0, 0.0
    for po, pm, pl_ in parts:
        factor = jnp.exp(pm - m)
        o = o + po * factor
        l = l + pl_ * factor
    return o, m, l


def kernel(
    res_h, gain_h, q_h, k_h, v_h, nkv_h, lens_h, ow_h, gw_h, uw_h, dw_h,
    out_ref,
    res_v, gain_v, q_v, k_v, v_v, nkv_v, lens_s, ow_v, gw_v, uw_v, dw_v,
    row_send, row_recv, col_send, col_recv, side_send, side_recv,
    proj_send, proj_recv, norm_send, norm_recv, pass_recv, far_recv, pair_send, pair_recv, down_send, down_recv, last_send, last_recv,
    load_sem, send_sem, recv_sem, norm_sem, pair_sem, side_sem,
):
    kvp = lax.axis_index("kvp")
    z = lax.axis_index("tp")
    x = kvp // (Y * C)
    y = lax.rem(kvp // C, Y)
    c = lax.rem(kvp, C)
    xs = [x] + [lax.rem(x + d, X) for d in range(1, X)]
    ys = [y] + [lax.rem(y + d, Y) for d in range(1, Y)]
    cs = [c, 1 - c]
    zs = [z] + [lax.rem(z + d, Z) for d in range(1, Z)]

    def index(o):
        return (xs[o[0]] * Y + ys[o[1]]) * C + cs[o[2]]

    def origin(o):
        return index(((X - o[0]) % X, (Y - o[1]) % Y, (C - o[2]) % C))

    small = [(k_h, k_v), (q_h, q_v), (v_h, v_v), (nkv_h, nkv_v), (lens_h, lens_s), (res_h, res_v), (gain_h, gain_v)]
    large = [(ow_h, ow_v), (gw_h, gw_v), (uw_h, uw_v), (dw_h, dw_v)]
    small = [pltpu.make_async_copy(s, d, load_sem.at[i]) for i, (s, d) in enumerate(small)]
    large = [pltpu.make_async_copy(s, d, load_sem.at[7 + i]) for i, (s, d) in enumerate(large)]
    for copy in small:
        copy.start()

    barrier = pltpu.get_barrier_semaphore()
    for o in GREET:
        pl.semaphore_signal(barrier, inc=1, device_id=(index(o), zs[o[3]]), device_id_type=MESH)

    for copy in small:
        copy.wait()
    for copy in large:
        copy.start()

    scale = 1.0 / math.sqrt(128)
    ri = lax.broadcasted_iota(jnp.int32, (128, 128), 0)
    li = lax.broadcasted_iota(jnp.int32, (128, 128), 1)
    perm = (li == (ri & 7) * 16 + (ri >> 3)).astype(BF)
    q = jnp.dot(perm, q_v[...].reshape(128, 128), preferred_element_type=F32)
    qm = jnp.concatenate([jnp.where((ri & 7) == b, q, 0.0).astype(BF) for b in range(8)], axis=1)
    kc = jnp.concatenate([k_v[b] for b in range(8)], axis=1)
    nkv = nkv_v[...].astype(F32)
    nk = nkv[:, 0, :]
    nv = nkv[:, 1, :]
    nkc = jnp.concatenate([jnp.broadcast_to(nk[b : b + 1], (8, 128)) for b in range(8)], axis=1).astype(BF)
    contract = (((1,), (1,)), ((), ()))
    s = lax.dot_general(kc, qm, contract, preferred_element_type=F32) * scale
    fresh = lax.dot_general(nkc, qm, contract, preferred_element_type=F32)[0:1] * scale
    lane = lax.broadcasted_iota(jnp.int32, (1, 128), 1) & 7
    limit = functools.reduce(lambda a, b: jnp.where(lane == b, lens_s[b], a), range(1, 8), jnp.full((1, 128), lens_s[0]))
    live = (ri + kvp * 128) < limit
    mine = (jnp.zeros((1, 128), jnp.int32) + kvp) == 0
    s = jnp.where(live, s, EMPTY)
    fresh = jnp.where(mine, fresh, EMPTY)
    m = jnp.maximum(jnp.max(s, axis=0, keepdims=True), fresh)
    m = m.astype(BF).astype(F32)
    p = jnp.where(live, jnp.exp(s - m), 0.0)
    pf = jnp.where(mine, jnp.exp(fresh - m), 0.0)
    l = jnp.sum(p, axis=0, keepdims=True) + pf
    pm = jnp.concatenate([jnp.where((li & 7) == b, p, 0.0).astype(BF) for b in range(8)], axis=0)
    vt = jnp.concatenate([v_v[b].T for b in range(8)], axis=1)
    o = jnp.dot(vt, pm, preferred_element_type=F32)
    ri8 = lax.broadcasted_iota(jnp.int32, (8, 128), 0)
    li8 = lax.broadcasted_iota(jnp.int32, (8, 128), 1)
    pfm = jnp.where((li8 & 7) == ri8, pf, 0.0)
    pad = jnp.zeros((120, 128), F32)
    nvt = jnp.concatenate([nv, pad], axis=0).T.astype(BF)
    o = o + jnp.dot(nvt, jnp.concatenate([pfm, pad], axis=0).astype(BF), preferred_element_type=F32)
    pack(row_send.at[0], o[0:64], m, l)
    pack(row_send.at[1], o[64:128], m, l)
    side_send[...] = jnp.concatenate(
        [res_v[...], jnp.broadcast_to(gain_v[...].astype(F32).reshape(1, 64), (8, 64)).astype(BF)], axis=1
    )

    pl.semaphore_wait(barrier, len(GREET))

    def send(src, dst, sends, recvs, device):
        pltpu.make_async_remote_copy(src, dst, sends, recvs, device_id=device, device_id_type=MESH).start()

    def whole(ref, sem):
        pltpu.make_async_copy(ref, ref, sem).wait()

    for j, o_ in enumerate(ROW):
        send(row_send.at[cs[o_[2]]], row_recv.at[j], send_sem.at[0], recv_sem.at[0], (index(o_), z))
    for j, dz in enumerate(DEPTH):
        if min(dz, Z - dz) <= 2:
            send(side_send, side_recv.at[j], send_sem.at[0], side_sem.at[0], (kvp, zs[dz]))
    whole(row_recv, recv_sem.at[0])
    o, m, l = combine([unpack(row_send[c])] + [unpack(row_recv[j]) for j in range(len(ROW))])
    pack(col_send, o, m, l)

    for j, o_ in enumerate(COL):
        send(col_send, col_recv.at[j], send_sem.at[0], recv_sem.at[2], (index(o_), z))
    whole(side_recv.at[pl.ds(3, 4)], side_sem.at[0])
    for j, dz in enumerate(DEPTH):
        if min(dz, Z - dz) > 2:
            send(side_send, side_recv.at[j], send_sem.at[0], side_sem.at[1], (kvp, zs[dz]))
    whole(side_recv.at[pl.ds(0, 3)], side_sem.at[1])
    lane8 = lax.broadcasted_iota(jnp.int32, (8, 128), 1)
    low = lane8 < 64
    side = [side_send[...].astype(F32)] + [side_recv[j].astype(F32) for j in range(Z - 1)]
    owner = [z] + [zs[Z - dz] for dz in DEPTH]
    res_parts, gain_parts = [], []
    for g in range(Z // 2):
        r, gn = jnp.zeros((8, 128), F32), jnp.zeros((8, 128), F32)
        for t, own in zip(side, owner):
            turned = pltpu.roll(t, 64, 1)
            here = (jnp.zeros((8, 128), jnp.int32) + own) == jnp.where(low, 2 * g, 2 * g + 1)
            r = jnp.where(here, jnp.where(low, t, turned), r)
            gn = jnp.where(here, jnp.where(low, turned, t), gn)
        res_parts.append(r)
        gain_parts.append(gn)
    res = jnp.concatenate(res_parts, axis=1)
    gain = jnp.concatenate(gain_parts, axis=1)
    whole(col_recv, recv_sem.at[2])
    own = [unpack(col_send[...])] + [unpack(col_recv[j]) for j, o_ in enumerate(COL) if o_[2] == 0]
    other = [unpack(col_recv[j]) for j, o_ in enumerate(COL) if o_[2] == 1]
    o, _, l = combine(own)
    own = o / l
    o, _, l = combine(other)
    other = o / l
    first = (jnp.zeros((64, 128), jnp.int32) + c) == 0
    att = jnp.concatenate([jnp.where(first, own, other), jnp.where(first, other, own)], axis=0).T
    att = jnp.concatenate([att[8 * h : 8 * h + 8] for h in range(16)], axis=1).astype(BF)

    large[0].wait()
    part = jnp.dot(att, ow_v[...], preferred_element_type=F32)
    proj_send[...] = part.astype(BF)
    for j, dz in enumerate(DEPTH):
        send(proj_send, proj_recv.at[j], send_sem.at[0], recv_sem.at[3], (kvp, zs[dz]))
    whole(proj_recv, recv_sem.at[3])
    total = part
    for j in range(Z - 1):
        total = total + proj_recv[j].astype(F32)
    hidden = (res + total).astype(BF).astype(F32)
    square = jnp.sum(hidden * hidden, axis=1, keepdims=True)
    high = square.astype(BF).astype(F32)
    norm_send[:, pl.ds(0, 512)] = (hidden * gain).astype(BF)
    norm_send[:, pl.ds(512, 128)] = jnp.where(low, high, square - high).astype(BF)

    n = len(NEAR)
    sibling = (index((0, 0, 1)), z)
    span_of = lambda spans, j: max(k for k, (lo, _) in enumerate(spans) if lo <= j)
    for j, o_ in enumerate(NEAR):
        send(norm_send, norm_recv.at[j], send_sem.at[0], norm_sem.at[span_of(NEAR_SPANS, j)], (index(o_), z))
    for j, o_ in enumerate(FAR):
        send(norm_send, far_recv.at[j], send_sem.at[0], norm_sem.at[2 + span_of(FAR_SPANS, j)], (index(o_), z))
    send(norm_send, pass_recv.at[n], send_sem.at[0], norm_sem.at[3], sibling)
    for copy in large[1:3]:
        copy.wait()

    def gate_up(ref, block, gate, up):
        feats = ref[:, pl.ds(0, 512)]
        cols = pl.ds(pl.multiple_of(block * 512, 512), 512)
        gate = gate + lax.dot_general(feats, gw_v[:, cols], contract, preferred_element_type=F32)
        up = up + lax.dot_general(feats, uw_v[:, cols], contract, preferred_element_type=F32)
        return gate, up, ref[:, pl.ds(512, 128)].astype(F32)

    gate = jnp.zeros((8, 104), F32)
    up = jnp.zeros((8, 104), F32)
    gate, up, squares = gate_up(norm_send, kvp, gate, up)
    for k, (lo, hi) in reversed(list(enumerate(NEAR_SPANS))):
        slots = norm_recv.at[pl.ds(lo, hi - lo)]
        whole(slots, norm_sem.at[k])
        send(slots, pass_recv.at[pl.ds(lo, hi - lo)], send_sem.at[0], norm_sem.at[4 + k], sibling)
        for j in reversed(range(lo, hi)):
            gate, up, extra = gate_up(norm_recv.at[j], origin(NEAR[j]), gate, up)
            squares = squares + extra
    whole(pass_recv.at[n], norm_sem.at[3])
    gate, up, extra = gate_up(pass_recv.at[n], origin((0, 0, 1)), gate, up)
    squares = squares + extra
    for k, (lo, hi) in reversed(list(enumerate(NEAR_SPANS))):
        whole(pass_recv.at[pl.ds(lo, hi - lo)], norm_sem.at[4 + k])
        for j in reversed(range(lo, hi)):
            gate, up, extra = gate_up(pass_recv.at[j], origin((NEAR[j][0], NEAR[j][1], 1)), gate, up)
            squares = squares + extra
    for k, (lo, hi) in reversed(list(enumerate(FAR_SPANS))):
        whole(far_recv.at[pl.ds(lo, hi - lo)], norm_sem.at[2 + k])
        for j in reversed(range(lo, hi)):
            gate, up, extra = gate_up(far_recv.at[j], origin(FAR[j]), gate, up)
            squares = squares + extra
    squares = squares[:, 0:1] + squares[:, 64:65]
    inverse = lax.rsqrt(squares * (1.0 / D) + EPS)
    gate = gate * inverse
    up = up * inverse
    inner = (gate / (1.0 + jnp.exp(-gate)) * up).astype(BF)

    large[3].wait()

    def down(block):
        cols = pl.ds(pl.multiple_of(block * 512, 512), 512)
        return jnp.dot(inner, dw_v[:, cols], preferred_element_type=F32)

    n = len(CHIPS)
    order = CHIPS + [(0, 0, 0)]
    sibling = (index((0, 0, 1)), z)
    for g in range(len(order) // GROUP):
        for j in range(GROUP * g, GROUP * g + GROUP):
            pair_send[j] = down(index((order[j][0], order[j][1], 1))).astype(BF)
        slots = pl.ds(GROUP * g, GROUP)
        send(pair_send.at[slots], pair_recv.at[slots], send_sem.at[0], pair_sem.at[g], sibling)
    for g in range(len(order) // GROUP):
        js = range(GROUP * g, GROUP * g + GROUP)
        blocks = [down(index(order[j])) for j in js]
        whole(pair_recv.at[pl.ds(GROUP * g, GROUP)], pair_sem.at[g])
        for j, block in zip(js, blocks):
            total = block + pair_recv[j].astype(F32)
            if j < n:
                down_send[j] = total.astype(BF)
                send(down_send.at[j], down_recv.at[j], send_sem.at[0], recv_sem.at[4], (index(order[j]), z))
    whole(down_recv, recv_sem.at[4])
    for j in range(n):
        total = total + down_recv[j].astype(F32)

    for g in range(Z // 2):
        last_send[g] = total[:, 128 * g : 128 * g + 128]
    for j, dz in enumerate(DEPTH):
        send(last_send.at[zs[dz] // 2], last_recv.at[j], send_sem.at[0], recv_sem.at[1], (kvp, zs[dz]))
    mine = last_send[z // 2]
    hid = jnp.zeros((8, 128), F32)
    for g in range(Z // 2):
        hid = jnp.where((jnp.zeros((8, 128), jnp.int32) + z // 2) == g, hidden[:, 128 * g : 128 * g + 128], hid)
    whole(last_recv, recv_sem.at[1])
    for j in range(Z - 1):
        mine = mine + last_recv[j]
    mine = mine + hid
    odd = (jnp.zeros((8, 128), jnp.int32) + lax.rem(z, 2)) == 1
    mine = jnp.where(odd, pltpu.roll(mine, 64, 1), mine)
    out_ref[...] = mine[:, 0:64].astype(BF)

    for ref in (row_recv, side_recv, col_recv, proj_recv, norm_recv, pair_recv, last_recv, down_recv, far_recv):
        whole(ref, send_sem.at[0])
    whole(pass_recv, send_sem.at[0])


def local(residual, norm_gain, queries, keys, values, new_kv, lens, out_weight, gate_weight, up_weight, down_weight):
    V = pltpu.VMEM
    n, far = len(NEAR), len(FAR)
    scratch = [
        V((8, 64), BF), V((64,), BF), V((8, 16, 128), BF), V((8, 128, 128), BF), V((8, 128, 128), BF),
        V((8, 2, 128), BF), pltpu.SMEM((8,), jnp.int32), V((2048, 512), BF),
        V((104, D), BF), V((104, D), BF), V((104, D), BF),
        V((2, 9, 8, 128), BF), V((7, 9, 8, 128), BF), V((9, 8, 128), BF), V((7, 9, 8, 128), BF),
        V((8, 128), BF), V((7, 8, 128), BF),
        V((8, 512), BF), V((7, 8, 512), BF),
        V((8, 640), BF), V((n, 8, 640), BF), V((n + 1, 8, 640), BF), V((far, 8, 640), BF),
        V((16, 8, 512), BF), V((16, 8, 512), BF),
        V((len(CHIPS), 8, 512), BF), V((len(CHIPS), 8, 512), BF), V((4, 8, 128), F32), V((7, 8, 128), F32),
        pltpu.SemaphoreType.DMA((11,)), pltpu.SemaphoreType.DMA((1,)), pltpu.SemaphoreType.DMA((5,)),
        pltpu.SemaphoreType.DMA((6,)), pltpu.SemaphoreType.DMA((2,)), pltpu.SemaphoreType.DMA((2,)),
    ]
    return pl.pallas_call(
        kernel,
        name="decode_step",
        out_shape=jax.ShapeDtypeStruct((8, 64), BF),
        in_specs=[pl.BlockSpec(memory_space=pltpu.HBM)] * 11,
        out_specs=pl.BlockSpec(memory_space=pltpu.VMEM),
        scratch_shapes=scratch,
        cost_estimate=pl.CostEstimate(flops=120_000_000, bytes_accessed=13_000_000, transcendentals=20_000),
        compiler_params=pltpu.CompilerParams(collective_id=0, has_side_effects=True, vmem_limit_bytes=60 << 20),
    )(
        residual, norm_gain, queries, keys.reshape(8, 128, 128), values.reshape(8, 128, 128),
        new_kv.reshape(8, 2, 128), lens, out_weight, gate_weight, up_weight, down_weight,
    )


def solution(mesh):
    in_specs = (
        P(None, ("kvp", "tp")),
        P(("kvp", "tp")),
        P(None, "tp", None),
        P(None, "kvp", "tp", None),
        P(None, "kvp", "tp", None),
        P(None, None, "tp", None),
        P(),
        P("tp", "kvp"),
        P(("kvp", "tp"), None),
        P(("kvp", "tp"), None),
        P(("kvp", "tp"), None),
    )
    out_specs = P(None, ("kvp", "tp"))
    return jax.shard_map(local, mesh=mesh, in_specs=in_specs, out_specs=out_specs, check_vma=False)
```
